128 devices in a mesh: wide: 8 (over x, core), sixteen: 16 (over y, z).
Axes of the slice: x: 4, y: 4, z: 4, core: 2. Of those that a mesh axis runs over, the one named last changes fastest.
Arguments:
- features: float32 [8, 16, 512, 128], P('wide', 'sixteen'), may hold values from -6 to 6
- positions: float32 [8, 16, 3, 512], P('wide', 'sixteen'), may hold values from 0 to 1, as said below
- tile_lists: int32 [8, 16, 4, 16], P('wide', 'sixteen'), may hold values from 0 to 36, as said below
- value_proj: float32 [128, 128], replicated, may hold values from -0.5 to 0.5
- radial_mix: float32 [16, 128], replicated, may hold values from -1.5 to 1.5
- charge_proj: float32 [128, 128], replicated, may hold values from -0.5 to 0.5
- screening: float32 [128], P(('wide', 'sixteen')), may hold values from 20 to 200
- smearing: float32 [128], P(('wide', 'sixteen')), may hold values from 0.003 to 0.02
- mesh_gain: float32 [128], replicated, may hold values from 0.25 to 1.75
- mesh_up: float32 [128, 256], replicated, may hold values from -0.5 to 0.5
- mesh_down: float32 [256, 128], replicated, may hold values from -0.375 to 0.375
- long_proj: float32 [128, 128], replicated, may hold values from -0.5 to 0.5
- atom_gain: float32 [128], replicated, may hold values from 0.25 to 1.75
- atom_up: float32 [128, 256], replicated, may hold values from -0.5 to 0.5
- atom_down: float32 [256, 128], replicated, may hold values from -0.375 to 0.375
Outputs:
- updated: float32 [8, 16, 512, 128], P('wide', 'sixteen')
The draws below stay inside these ranges and needn't reach their ends.
Inputs may be any that keep to these rules, and one draw needn't show every extreme that they name: `tile_lists`: each list of tile t of a block holds codes nb * 4 + t2 of tiles of the 3 x 3 blocks around it with (t2 - t) mod 4 equal to 0, 1 or 3; its first entry is the tile itself, 16 + t; its live entries are distinct; empty entries hold 36 and stand after all live ones; every list has 1 to 16 live entries and some list has 16. `positions`: the third coordinate of atom a of a block lies between a / 512 and (a + 1) / 512.
All inputs are finite; a program needn't handle non-finite values.
Results may differ from the reference program's by a relative error of at most 0.0003.
Values sent between devices are 32-bit elements; how exact they have to be, the bound alone decides.
No kernel may reach another device: no remote copies, remote signals or barrier semaphores. Data moves between devices by JAX's collectives and lax.ppermute only.
A program may use at most 64 MiB of HBM per device.

```python
import math
import jax
import jax.numpy as jnp
from jax import lax

F = 128
C = 128
NB = 16
MESH = 64
HM = 256
FH = 256
TILE = 128
K = 16
ATOM_DEV = 512
BLOCKS_W = 8
BLOCKS_S = 16
N_WIDE = 8
N_SIXTEEN = 16


def draw_positions(key, part):
    key_plane = jax.random.fold_in(key, 21)
    key_depth = jax.random.fold_in(key, 22)
    plane = jax.random.uniform(key_plane, (BLOCKS_W, BLOCKS_S, 2, ATOM_DEV), jnp.float32)
    jitter = jax.random.uniform(key_depth, (BLOCKS_W, BLOCKS_S, 1, ATOM_DEV), jnp.float32)
    ranks = jnp.arange(ATOM_DEV).astype(jnp.float32)
    depth = (ranks[None, None, None, :] + jitter) / ATOM_DEV
    depth = jnp.minimum(depth, 1.0)
    return jnp.concatenate([plane, depth], axis=2).astype(jnp.float32)


def draw_tile_lists(key, part):
    tiles_per = ATOM_DEV // TILE
    empty_code = 9 * tiles_per
    blocks = BLOCKS_W * BLOCKS_S
    key_busy = jax.random.fold_in(key, 11)
    key_count = jax.random.fold_in(key, 12)
    key_score = jax.random.fold_in(key, 13)
    busy_level = jax.random.randint(key_busy, (blocks, 1), 0, 4)
    counts = 1 + jax.random.randint(key_count, (blocks, tiles_per), 0, K) // (1 + busy_level)
    counts = counts.at[0, 0].set(K)
    code_range = jnp.arange(empty_code, dtype=jnp.int32)
    code_tile = code_range % tiles_per
    own_tile = jnp.arange(tiles_per, dtype=jnp.int32)
    gap = (code_tile[None, :] - own_tile[:, None]) % tiles_per
    is_near = (gap == 0) | (gap == 1) | (gap == tiles_per - 1)
    scores = jax.random.randint(key_score, (blocks, tiles_per, empty_code), 0, 65536) * empty_code + code_range
    own_codes = 4 * tiles_per + own_tile
    is_own = code_range[None, None, :] == own_codes[None, :, None]
    scores = jnp.where(is_near[None] & ~is_own, scores, -1)
    picked = lax.top_k(scores, K - 1)[1].astype(jnp.int32)
    first_codes = jnp.broadcast_to(own_codes[None, :, None], (blocks, tiles_per, 1))
    tile_codes = jnp.concatenate([first_codes, picked], axis=2)
    slot_index = jnp.arange(K, dtype=jnp.int32)
    tile_codes = jnp.where(slot_index[None, None, :] < counts[:, :, None], tile_codes, empty_code)
    return tile_codes.reshape(BLOCKS_W, BLOCKS_S, tiles_per, K).astype(jnp.int32)


def block_levels(key, dims, split, low, top_value):
    loudness = 1.0
    for axis_at, shards_of in split:
        steps = jax.random.uniform(jax.random.fold_in(jax.random.fold_in(key, 6), axis_at), (shards_of,), jnp.float32, low / len(split), top_value / len(split))
        loudness = loudness * jnp.repeat(jnp.exp(steps), dims[axis_at] // shards_of).reshape((-1,) + (1,) * (len(dims) - 1 - axis_at))
    return loudness


def bell_draw(own_key, extent, scale, reach, split=(), kind=jnp.bfloat16):
    array = jax.random.normal(own_key, extent, jnp.float32) * scale
    if len(split) > 0:
        array = block_levels(own_key, extent, split, -0.22, 0.18) * array
    return jnp.clip(array, min=-reach, max=reach).astype(kind)


def setup_inputs(seed: int = 0) -> dict:
    splits = jax.random.split(jax.random.key(seed), 16)
    return {
        "features": bell_draw(splits[0], (BLOCKS_W, BLOCKS_S, ATOM_DEV, F), 1.0, 6.0, ((0, 8), (1, 16)), jnp.float32),
        "positions": draw_positions(jax.random.fold_in(splits[15], 71), 0),
        "tile_lists": draw_tile_lists(jax.random.fold_in(splits[15], 71), 0),
        "value_proj": bell_draw(splits[3], (F, F), F ** -0.5, 0.5, (), jnp.float32),
        "radial_mix": bell_draw(splits[4], (NB, F), NB ** -0.5, 1.5, (), jnp.float32),
        "charge_proj": bell_draw(splits[5], (F, C), F ** -0.5, 0.5, (), jnp.float32),
        "screening": jnp.clip(jnp.exp(math.log(200.0) - 2.3025851 * jax.random.uniform(splits[6], (C,), jnp.float32) ** block_levels(splits[6], (C,), ((0, 128),), -0.2, 0.2)), 20.0, 200.0),
        "smearing": jnp.clip(jnp.exp(math.log(0.02) - 1.89712 * jax.random.uniform(splits[7], (C,), jnp.float32) ** block_levels(splits[7], (C,), ((0, 128),), -0.2, 0.2)), 0.003, 0.02),
        "mesh_gain": jnp.clip(1.0 + 0.15 * jax.random.normal(splits[8], (C,), jnp.float32), 0.25, 1.75),
        "mesh_up": bell_draw(splits[9], (C, HM), C ** -0.5, 0.5, (), jnp.float32),
        "mesh_down": bell_draw(splits[10], (HM, C), HM ** -0.5, 0.375, (), jnp.float32),
        "long_proj": bell_draw(splits[11], (C, F), C ** -0.5, 0.5, (), jnp.float32),
        "atom_gain": jnp.clip(1.0 + 0.15 * jax.random.normal(splits[12], (F,), jnp.float32), 0.25, 1.75),
        "atom_up": bell_draw(splits[13], (F, FH), F ** -0.5, 0.5, (), jnp.float32),
        "atom_down": bell_draw(splits[14], (FH, F), FH ** -0.5, 0.375, (), jnp.float32),
    }


exact = lax.Precision.HIGHEST

def short_range(near_values, near_positions, tile_codes, radial_mix, wide_count, sixteen_count):
    atom_count = near_values.shape[2]
    feature_width = near_values.shape[3]
    tiles_per = atom_count // TILE
    basis_count = radial_mix.shape[0]
    empty_code = 9 * tiles_per
    cutoff = 0.8 / max(wide_count, sixteen_count)
    sharpness = 0.5 * (basis_count - 1) ** 2
    centres = jnp.arange(basis_count).astype(jnp.float32) / (basis_count - 1)
    offsets = jnp.arange(3).astype(jnp.float32) - 1.0
    global_x = (near_positions[:, :, 0, :] + offsets[:, None, None]) / wide_count
    global_y = (near_positions[:, :, 1, :] + offsets[None, :, None]) / sixteen_count
    global_z = near_positions[:, :, 2, :]
    placed = jnp.stack([global_x, global_y, global_z], axis=2)
    source_pos = placed.reshape(9, 3, tiles_per, TILE).transpose(0, 2, 1, 3).reshape(empty_code, 3, TILE)
    source_val = near_values.reshape(empty_code, TILE, feature_width)
    own_pos = source_pos[4 * tiles_per:5 * tiles_per]
    own_codes = 4 * tiles_per + jnp.arange(tiles_per, dtype=jnp.int32)
    diagonal = jnp.eye(TILE, dtype=bool)

    def one_slot(slot_index, running):
        slot_codes = tile_codes[:, slot_index]
        is_live = slot_codes < empty_code
        chosen = jnp.minimum(slot_codes, empty_code - 1)
        other_pos = source_pos[chosen]
        other_val = source_val[chosen]
        offset_vec = other_pos[:, :, None, :] - own_pos[:, :, :, None]
        delta_z = offset_vec[:, 2] - jnp.floor(offset_vec[:, 2] + 0.5)
        radius = jnp.sqrt(offset_vec[:, 0] ** 2 + offset_vec[:, 1] ** 2 + delta_z ** 2) / cutoff
        envelope = jnp.where(radius < 1.0, 0.5 * (jnp.cos(jnp.pi * radius) + 1.0), 0.0)
        itself = (slot_codes == own_codes)[:, None, None] & diagonal[None]
        envelope = jnp.where(is_live[:, None, None] & ~itself, envelope, 0.0)
        basis_vals = jnp.exp(-sharpness * (radius[:, None] - centres[None, :, None, None]) ** 2) * envelope[:, None]
        partial_sum = jnp.einsum('tbij,tjc->tbic', basis_vals, other_val, precision=exact)
        return running + jnp.einsum('tbic,bc->tic', partial_sum, radial_mix, precision=exact)
    running = lax.fori_loop(0, tile_codes.shape[1], one_slot, jnp.zeros((tiles_per, TILE, feature_width), jnp.float32))
    return running.reshape(atom_count, feature_width)

def stencil(coords):
    floored = jnp.floor(coords)
    fraction = coords - floored
    base_cell = floored.astype(jnp.int32)
    cell_list = []
    weights = []
    for corner in range(8):
        corner_steps = (corner // 4, corner // 2 % 2, corner % 2)
        cell_index = jnp.zeros(coords.shape[1], jnp.int32)
        weight = jnp.ones(coords.shape[1], jnp.float32)
        for dimension in range(3):
            cell_index = cell_index * MESH + (base_cell[dimension] + corner_steps[dimension]) % MESH
            if corner_steps[dimension]:
                weight = weight * fraction[dimension]
            else:
                weight = weight * (1.0 - fraction[dimension])
        cell_list.append(cell_index)
        weights.append(weight)
    return (cell_list, weights)

def filter_kernel(screening, smearing):
    sample_index = jnp.arange(MESH, dtype=jnp.int32)
    signed = jnp.where(sample_index < MESH // 2, sample_index, sample_index - MESH).astype(jnp.float32)
    wavenumber = 2.0 * jnp.pi * signed
    squares = wavenumber[:, None, None] ** 2 + wavenumber[None, :, None] ** 2 + wavenumber[None, None, :] ** 2
    kappa_sq = screening[:, None, None, None] ** 2
    return kappa_sq * jnp.exp(-0.5 * squares[None] * smearing[:, None, None, None] ** 2) / (squares[None] + kappa_sq)

def mesh_mlp(by_cells, mesh_gain, mesh_up, mesh_down):
    inverse_rms = lax.rsqrt(lax.optimization_barrier(jnp.mean(by_cells ** 2, axis=0, keepdims=True)) + 1e-06)
    normed = by_cells * inverse_rms * mesh_gain[:, None]
    hidden = jax.nn.silu(jnp.einsum('ch,cn->hn', mesh_up, normed, precision=exact))
    return jnp.einsum('hc,hn->cn', mesh_down, hidden, precision=exact)

def reference(features, positions, tile_lists, value_proj, radial_mix, charge_proj, screening, smearing, mesh_gain, mesh_up, mesh_down, long_proj, atom_gain, atom_up, atom_down):
    wide_count = N_WIDE
    sixteen_count = N_SIXTEEN
    devices = wide_count * sixteen_count
    atom_count = features.shape[2]
    feature_width = features.shape[3]
    channels = charge_proj.shape[1]
    cells_total = MESH ** 3
    values = jnp.einsum('xyaf,fg->xyag', features, value_proj, precision=exact)

    def one_block(block_index):
        row_index = block_index // sixteen_count
        column = block_index % sixteen_count
        row_list = (row_index + jnp.arange(3, dtype=jnp.int32) - 1) % wide_count
        column_list = (column + jnp.arange(3, dtype=jnp.int32) - 1) % sixteen_count
        near_values = values[row_list][:, column_list]
        near_positions = positions[row_list][:, column_list]
        return short_range(near_values, near_positions, tile_lists[row_index, column], radial_mix, wide_count, sixteen_count)
    messages = lax.map(one_block, jnp.arange(devices, dtype=jnp.int32)).reshape(devices * atom_count, feature_width)
    flat_features = features.reshape(devices * atom_count, feature_width)
    charges = jnp.dot(flat_features, charge_proj, precision=exact)
    block_x = jnp.arange(wide_count).astype(jnp.float32)
    block_y = jnp.arange(sixteen_count).astype(jnp.float32)
    coords_x = ((block_x[:, None, None] + positions[:, :, 0, :]) * (MESH / wide_count)).reshape(-1)
    coords_y = ((block_y[None, :, None] + positions[:, :, 1, :]) * (MESH / sixteen_count)).reshape(-1)
    coords_z = (positions[:, :, 2, :] * MESH).reshape(-1)
    cell_list, weights = stencil(jnp.stack([coords_x, coords_y, coords_z]))
    density = jnp.zeros((cells_total, channels), jnp.float32)
    for corner in range(8):
        density = density.at[cell_list[corner]].add(weights[corner][:, None] * charges)
    field_all = density.T.reshape(channels, MESH, MESH, MESH)

    def smooth(channel_item):
        field_grid, kappa_value, sigma_value = channel_item
        kernel = filter_kernel(kappa_value[None], sigma_value[None])[0]
        return jnp.real(jnp.fft.ifftn(jnp.fft.fftn(field_grid) * kernel))
    potential = lax.map(smooth, (field_all, screening, smearing)).reshape(channels, cells_total)
    blocks_view = potential.reshape(channels, devices, cells_total // devices).transpose(1, 0, 2)
    mesh_out = lax.map(lambda block_view: mesh_mlp(block_view, mesh_gain, mesh_up, mesh_down), blocks_view)
    mesh_out = mesh_out.transpose(1, 0, 2).reshape(channels, cells_total)
    at_atoms = jnp.zeros((channels, devices * atom_count), jnp.float32)
    for corner in range(8):
        at_atoms = at_atoms + weights[corner][None, :] * mesh_out[:, cell_list[corner]]
    long_terms = jnp.einsum('cn,cf->nf', at_atoms, long_proj, precision=exact)
    summed = flat_features + messages + long_terms
    inverse_rms = lax.rsqrt(lax.optimization_barrier(jnp.mean(summed ** 2, axis=-1, keepdims=True)) + 1e-06)
    normed = summed * inverse_rms * atom_gain
    hidden = jax.nn.silu(jnp.dot(normed, atom_up, precision=exact))
    updated = summed + jnp.dot(hidden, atom_down, precision=exact)
    return updated.reshape(wide_count, sixteen_count, atom_count, feature_width)
```

```python
import functools
import math

import jax
import jax.numpy as jnp
import ml_dtypes
import numpy as np
from jax import lax
from jax.experimental import pallas as pl
from jax.experimental.pallas import tpu as pltpu
from jax.sharding import PartitionSpec as P

F32 = jnp.float32
BF = jnp.bfloat16
MESH = 64
LANES = 128
ATOMS = 512
CHUNK = 64
CHUNKS = ATOMS // CHUNK
BASES = 16
ROWS = 24
PACK = 528
FAR = 1000.0
CUTOFF = 0.05
MID = 8
LIMIT = 48 * 1024 * 1024


def split(x):
    hi = x.astype(BF)
    return hi, (x - hi.astype(F32)).astype(BF)


def dot(a, b):
    return jnp.dot(a, b, preferred_element_type=F32)


def dot_nt(a, b):
    return lax.dot_general(a, b, (((1,), (1,)), ((), ())), preferred_element_type=F32)


def dot3(a, b):
    ah, al = split(a)
    bh, bl = split(b)
    return dot(ah, bh) + (dot(ah, bl) + dot(al, bh))


def lane_iota(shape):
    return lax.broadcasted_iota(jnp.int32, shape, len(shape) - 1)


def half_turn(x):
    return pltpu.roll(x, 64, x.ndim - 1)


def pack_body(feat_ref, pos_ref, proj_ref, out_ref):
    out_ref[0:ATOMS, :] = dot3(feat_ref[...], proj_ref[...])
    for d in range(3):
        for t in range(4):
            row = ATOMS + 4 * d + t
            out_ref[row : row + 1, :] = pos_ref[d : d + 1, t * LANES : (t + 1) * LANES]
    out_ref[ATOMS + 12 : PACK, :] = jnp.zeros((PACK - ATOMS - 12, LANES), F32)


class Hats:
    def __init__(self, pos):
        filled = jnp.concatenate([pos, jnp.zeros((5, ATOMS), F32)], axis=0)
        columns = filled.T
        wide = lambda d, scale: jnp.broadcast_to(columns[:, d : d + 1] * scale, (ATOMS, LANES))
        self.ux = wide(0, 8.0)
        self.uy = wide(1, 4.0)
        lane = lane_iota((1, LANES))
        self.half = (lane // 64).astype(F32)
        self.low = lane < 64
        depth = jnp.abs(wide(2, float(MESH)) - (lane % 64).astype(F32))
        self.hz = jnp.maximum(1.0 - jnp.minimum(depth, 64.0 - depth), 0.0)
        self.pairs = [self.y(2.0 * h + self.half) * self.hz for h in range(2)]
        self.top = self.y(4.0) * self.hz

    def x(self, cell):
        return jnp.maximum(1.0 - jnp.abs(self.ux - cell), 0.0)

    def y(self, cell):
        return jnp.maximum(1.0 - jnp.abs(self.uy - cell), 0.0)

    def row(self, r):
        if r < 16:
            return self.x(float(r % 8)) * self.pairs[r // 8]
        x = r - 16
        low = self.x(float(x)) * self.top
        if x < 4:
            high = self.x(8.0) * (self.y(float(x)) * self.hz)
        elif x == 4:
            high = self.x(8.0) * self.top
        else:
            high = 0.0
        return jnp.where(self.low, low, high)

    def two_rows(self, r):
        return split(jnp.concatenate([self.row(r), self.row(r + 1)], axis=1))


def spread_body(feat_ref, pos_ref, proj_ref, out_ref):
    charges = dot3(feat_ref[...], proj_ref[...])
    high, low = split(charges.T)
    both = jnp.concatenate([high, low], axis=0)
    hats = Hats(pos_ref[...])
    for r in range(0, ROWS, 2):
        wh, wl = hats.two_rows(r)
        first = dot(both, wh)
        result = (first[:LANES] + first[LANES:]) + dot(high, wl)
        for k in range(2):
            out_ref[pl.ds(r + k, LANES, stride=ROWS), :] = result[:, k * LANES : (k + 1) * LANES]


def real_basis():
    n = np.arange(MESH)
    rows = []
    for k in range(MESH):
        if k == 0:
            rows.append(np.full(MESH, 1.0 / 8.0))
        elif k == MESH // 2:
            rows.append(np.where(n % 2 == 0, 1.0, -1.0) / 8.0)
        elif k < MESH // 2:
            rows.append(np.cos(2 * np.pi * (k * n % MESH) / MESH) * math.sqrt(2.0) / 8.0)
        else:
            rows.append(np.sin(2 * np.pi * ((MESH - k) * n % MESH) / MESH) * math.sqrt(2.0) / 8.0)
    return np.stack(rows)


def halves(table):
    high = table.astype(np.float32).astype(ml_dtypes.bfloat16)
    low = (table - high.astype(np.float64)).astype(np.float32).astype(ml_dtypes.bfloat16)
    return high, low


def stacked(table):
    high, low = halves(table)
    return np.concatenate([high, low, high], axis=1)


def squared(table):
    high, low = halves(table)
    top = np.concatenate([high, low], axis=1)
    bottom = np.concatenate([high, np.zeros_like(low)], axis=1)
    return np.concatenate([top, bottom], axis=0)


def filter_tables():
    q = real_basis()
    y_forward = np.concatenate([q[:, 0::2], q[:, 1::2]], axis=0)
    y_back = np.concatenate([q.T[0::2], q.T[1::2]], axis=0)
    twice = np.kron(np.eye(2), q.T)
    return (
        stacked(q),
        stacked(y_forward),
        squared(twice),
        squared(twice.T),
        stacked(y_back),
        stacked(q.T),
    )


def stack_rows(x):
    high, low = split(x)
    return jnp.concatenate([high, high, low], axis=0)


def sum_halves(x):
    return x[:, :LANES] + x[:, LANES:]


def filter_body(
    screen_ref, smear_ref, in_ref, xf_ref, yf_ref, zf_ref, zb_ref, yb_ref, xb_ref, out_ref, turn_ref, edge_ref
):
    devices = 128
    low = lane_iota((1, LANES)) < 64
    place = lax.broadcasted_iota(jnp.int32, (devices, 1), 0) % 16

    side = [in_ref[pl.ds(16 + y, devices, stride=ROWS), :] for y in range(5)]
    corner = jnp.where(place == 0, pltpu.roll(side[4], 113, 0), pltpu.roll(side[4], 1, 0))
    side[0] = side[0] + corner
    for h in range(2):
        both = jnp.where(low, half_turn(side[2 * h]), side[2 * h + 1])
        edge_ref[h * devices : (h + 1) * devices, :] = pltpu.roll(both, 16, 0)

    first_row = lax.broadcasted_iota(jnp.int32, (8, 1), 0) == 0
    x_forward = xf_ref[...]
    for s in range(16):
        parts = []
        for h in range(2):
            tiles = []
            for w in range(8):
                at = w * 16 + s
                tile = in_ref[at * ROWS + h * 8 : at * ROWS + h * 8 + 8, :]
                edge = edge_ref[h * devices + at : h * devices + at + 1, :]
                tile = tile + jnp.where(first_row, edge, 0.0)
                if h == 0:
                    below = (w * 16 + (s + 15) % 16) * ROWS + 16
                    tile = tile + jnp.where(low, in_ref[below : below + 8, :], 0.0)
                tiles.append(tile)
            parts.append(jnp.concatenate(tiles, axis=0))
        result = dot(x_forward, stack_rows(jnp.concatenate(parts, axis=1)))
        for h in range(2):
            turn_ref[pl.ds(2 * s + h, MESH, stride=32), :] = result[:, h * LANES : (h + 1) * LANES]

    kappa = screen_ref[0]
    kappa_sq = kappa * kappa
    decay = -0.5 * smear_ref[0] * smear_ref[0]
    lane = lane_iota((1, LANES))
    fold = lambda k: jnp.minimum(k, MESH - k).astype(F32)
    nz = fold(lane % 64)
    ny = fold(lax.broadcasted_iota(jnp.int32, (MESH, 1), 0))
    scale = 4.0 * math.pi**2
    yz = (ny * ny + nz * nz) * scale
    y_forward, z_forward = yf_ref[...], zf_ref[...]
    z_back, y_back = zb_ref[...], yb_ref[...]
    group = 4
    for start in range(0, 32, group):
        planes = []
        for p in range(start, start + group):
            pair = jnp.concatenate(
                [turn_ref[(2 * p + k) * 32 : (2 * p + k + 1) * 32, :] for k in range(2)], axis=1
            )
            result = dot(y_forward, stack_rows(pair))
            a, b = result[:, :LANES], result[:, LANES:]
            straight = jnp.where(low, a[:MESH], b[MESH:])
            planes.append(straight + half_turn(jnp.where(low, b[:MESH], a[MESH:])))
        stack = jnp.concatenate(planes, axis=0)
        stack = sum_halves(dot(jnp.concatenate(split(stack), axis=1), z_forward))
        gains = []
        for p in range(start, start + group):
            nx = fold(2 * p + lane // 64)
            square = yz + nx * nx * scale
            gains.append(kappa_sq * jnp.exp(square * decay) / (square + kappa_sq))
        stack = stack * jnp.concatenate(gains, axis=0)
        stack = sum_halves(dot(jnp.concatenate(split(stack), axis=1), z_back))
        for g in range(0, group, 2):
            pair = jnp.concatenate([stack[(g + k) * MESH : (g + k + 1) * MESH] for k in range(2)], axis=1)
            result = dot(y_back, stack_rows(pair))
            for k in range(2):
                p = start + g + k
                a = result[:32, k * LANES : (k + 1) * LANES]
                b = result[32:, k * LANES : (k + 1) * LANES]
                turn_ref[2 * p * 32 : 2 * p * 32 + 32, :] = jnp.where(low, a, half_turn(b))
                turn_ref[2 * p * 32 + 32 : 2 * p * 32 + 64, :] = jnp.where(low, half_turn(a), b)

    x_back = xb_ref[...]
    for s in range(16):
        pair = jnp.concatenate(
            [turn_ref[pl.ds(2 * s + h, MESH, stride=32), :] for h in range(2)], axis=1
        )
        result = dot(x_back, stack_rows(pair))
        for w in range(8):
            at = (w * 16 + s) * ROWS
            for h in range(2):
                tile = result[w * 8 : (w + 1) * 8, h * LANES : (h + 1) * LANES]
                out_ref[at + h * 8 : at + h * 8 + 8, :] = tile
                if h == 0:
                    below = (w * 16 + (s + 15) % 16) * ROWS + 16
                    out_ref[below : below + 8, :] = jnp.where(low, tile, 0.0)

    ahead = [pltpu.roll(out_ref[pl.ds(8 * h, devices, stride=ROWS), :], 112, 0) for h in range(2)]
    turned = [half_turn(x) for x in ahead]
    corner = jnp.where(place == 15, pltpu.roll(turned[0], 15, 0), pltpu.roll(turned[0], 127, 0))
    for y, high in enumerate([turned[0], ahead[0], turned[1], ahead[1], corner]):
        rows = pl.ds(16 + y, devices, stride=ROWS)
        out_ref[rows, :] = jnp.where(low, out_ref[rows, :], high)


ENVELOPE = (
    0.9999999991137324,
    -0.4674010362718563,
    0.0945531128786198,
    -0.011119339660821159,
    0.0008600612678157039,
    -4.252312938118321e-05,
)


def short_body(live_ref, near_ref, left_ref, right_ref, mix_ref, out_ref, val_ref, win_ref, own_ref, sum_ref):
    lane = lane_iota((1, LANES))
    pos = near_ref[PACK + ATOMS : PACK + ATOMS + 16, :]
    for d, scale in ((0, 0.125), (1, 0.0625), (2, 1.0)):
        for t in range(4):
            row = pos[4 * d + t : 4 * d + t + 1, :] * scale
            own_ref[d * ATOMS + t * LANES : d * ATOMS + (t + 1) * LANES, :] = jnp.broadcast_to(
                row, (LANES, LANES)
            ).T

    for nb in range(9):
        dx, dy = nb // 3 - 1, nb % 3 - 1
        ref = (left_ref, near_ref, right_ref)[dx + 1]
        base = (dy + 1) * PACK
        high, low = split(ref[base : base + ATOMS, :])
        both = jnp.concatenate([high, low], axis=1)
        val_ref[nb, 32 : 32 + ATOMS, :] = both
        val_ref[nb, 0:32, :] = both[ATOMS - 32 :, :]
        val_ref[nb, ATOMS + 32 :, :] = both[:32, :]
        pos = ref[base + ATOMS : base + PACK, :]
        for m in range(CHUNKS):
            t = m // 2
            turned = pltpu.roll(pos, 32 if m % 2 == 0 else 96, 1)
            first, second = ((t + 3) % 4, t) if m % 2 == 0 else (t, (t + 1) % 4)
            from_first = lane < (32 if m % 2 == 0 else 96)
            for d in range(3):
                a = turned[4 * d + first : 4 * d + first + 1, :]
                b = turned[4 * d + second : 4 * d + second + 1, :]
                if d == 0:
                    row = (jnp.where(from_first, a, b) + float(dx)) * 0.125
                elif d == 1:
                    row = (jnp.where(from_first, a, b) + float(dy)) * 0.0625
                else:
                    if m == 0:
                        a = a - 1.0
                    if m == CHUNKS - 1:
                        b = b + 1.0
                    row = jnp.where(from_first, a, b)
                win_ref[nb, m, d : d + 1, :] = row

    me = lax.broadcasted_iota(jnp.int32, (CHUNK, LANES), 0) + 32
    itself = (me == lane_iota((CHUNK, LANES))).astype(F32)
    zero = jnp.zeros((LANES, LANES), BF)

    def chunk(m, carry):
        t = m // 2
        even = m % 2 == 0
        tile_a = jnp.where(even, (t + 3) % 4, t)
        tile_b = jnp.where(even, t, (t + 1) % 4)
        from_first = lane < jnp.where(even, 32, 96)
        sum_ref[...] = jnp.zeros_like(sum_ref)
        start = pl.multiple_of(m * CHUNK, CHUNK)

        def block(nb, carry):
            live_a = live_ref[t, nb * 4 + tile_a]
            live_b = live_ref[t, nb * 4 + tile_b]

            @pl.when(live_a + live_b > 0)
            def _():
                window = win_ref[nb, m]
                far_a = (1 - live_a).astype(F32) * FAR
                far_b = (1 - live_b).astype(F32) * FAR
                xj = window[0:1] + jnp.where(from_first, far_a, far_b)
                dx = xj - own_ref[pl.ds(start, CHUNK), :]
                dy = window[1:2] - own_ref[pl.ds(ATOMS + start, CHUNK), :]
                dz = window[2:3] - own_ref[pl.ds(2 * ATOMS + start, CHUNK), :]
                s = (dx * dx + dy * dy + dz * dz) * (1.0 / CUTOFF**2)
                s = jnp.maximum(s, itself * jnp.where(nb == 4, 1.0, 0.0))
                s = jnp.minimum(s, 1.0)
                q = s * lax.rsqrt(jnp.maximum(s, 1e-30))
                v = q * float(BASES - 1) - float(MID)
                env = jnp.full_like(s, ENVELOPE[-1])
                for c in ENVELOPE[-2::-1]:
                    env = env * s + c
                rest = 1.0 - s
                middle = jnp.exp(-0.5 * v * v) * (env * (rest * rest))
                up, down = jnp.exp(v), jnp.exp(-v)
                terms = [None] * BASES
                terms[MID] = middle
                for b in range(MID + 1, BASES):
                    terms[b] = terms[b - 1] * up
                for b in range(MID - 1, -1, -1):
                    terms[b] = terms[b + 1] * down
                lhs = jnp.concatenate([jnp.concatenate(split(x), axis=1) for x in terms], axis=0)
                values = val_ref[nb, pl.ds(start, LANES), :]
                rhs = jnp.concatenate(
                    [values, jnp.concatenate([values[:, :LANES], zero], axis=1)], axis=0
                )
                sum_ref[...] += sum_halves(dot(lhs, rhs))

            return carry

        lax.fori_loop(0, 9, block, 0)
        total = None
        for b in range(BASES):
            weight = mix_ref[b : b + 1, :] * math.exp(-0.5 * (b - MID) ** 2)
            term = sum_ref[b * CHUNK : (b + 1) * CHUNK, :] * weight
            total = term if total is None else total + term
        out_ref[pl.ds(start, CHUNK), :] = total
        return carry

    lax.fori_loop(0, CHUNKS, chunk, 0)


def silu(v):
    return v / (1.0 + jnp.exp(-v))


def stack_lanes(x):
    high, low = split(x)
    return jnp.concatenate([high, low, high], axis=1)


def final_body(
    feat_ref, pos_ref, msg_ref, in_ref, gain_ref, up_ref, down_ref, long_ref, again_ref, aup_ref, adown_ref, out_ref
):
    hats = Hats(pos_ref[...])
    up = stack_lanes(up_ref[...].T * gain_ref[...])
    down = stack_lanes(down_ref[...].T)
    at_atoms = jnp.zeros((ATOMS, LANES), F32)
    for r in range(0, ROWS, 2):
        cells = jnp.concatenate(
            [in_ref[pl.ds(r + k, LANES, stride=ROWS), :] for k in range(2)], axis=1
        )
        inverse = lax.rsqrt(jnp.mean(cells * cells, axis=0, keepdims=True) + 1e-06)
        hidden = silu(dot(up, stack_rows(cells * inverse)))
        mesh_out = dot(down, stack_rows(hidden))
        high, low = split(mesh_out)
        wh, wl = hats.two_rows(r)
        at_atoms = at_atoms + sum_halves(dot_nt(wh, jnp.concatenate([high, low], axis=0)))
        at_atoms = at_atoms + dot_nt(wl, high)
    summed = feat_ref[...] + msg_ref[...] + dot3(at_atoms, long_ref[...])
    inverse = lax.rsqrt(jnp.mean(summed * summed, axis=1, keepdims=True) + 1e-06)
    normed = summed * inverse * again_ref[...]
    hidden = silu(dot3(normed, aup_ref[...]))
    out_ref[...] = summed + dot3(hidden, adown_ref[...])


def whole():
    return pl.BlockSpec(memory_space=pltpu.VMEM)


def scalars():
    return pl.BlockSpec(memory_space=pltpu.SMEM)


def call(body, name, shape, in_specs, scratch, cost):
    return pl.pallas_call(
        body,
        out_shape=jax.ShapeDtypeStruct(shape, F32),
        in_specs=in_specs,
        out_specs=whole(),
        scratch_shapes=scratch,
        name=name,
        compiler_params=pltpu.CompilerParams(vmem_limit_bytes=LIMIT),
        cost_estimate=pl.CostEstimate(flops=cost, bytes_accessed=4 * 1024 * 1024, transcendentals=0),
    )


def pack_call(feat, pos, proj):
    return call(pack_body, "pack", (PACK, LANES), [whole()] * 3, [], 50_000_000)(feat, pos, proj)


def spread_call(feat, pos, proj):
    return call(spread_body, "spread", (LANES * ROWS, LANES), [whole()] * 3, [], 1_200_000_000)(
        feat, pos, proj
    )


def filter_call(screening, smearing, received):
    tables = [jnp.asarray(t) for t in filter_tables()]
    return call(
        filter_body,
        "filter",
        (LANES * ROWS, LANES),
        [scalars(), scalars()] + [whole()] * 7,
        [pltpu.VMEM((MESH * 32, LANES), F32), pltpu.VMEM((256, LANES), F32)],
        2_000_000_000,
    )(screening, smearing, received, *tables)


def short_call(live, near, left, right, mix):
    return call(
        short_body,
        "short_range",
        (ATOMS, LANES),
        [scalars()] + [whole()] * 4,
        [
            pltpu.VMEM((9, ATOMS + 64, 2 * LANES), BF),
            pltpu.VMEM((9, CHUNKS, 8, LANES), F32),
            pltpu.VMEM((3 * ATOMS, LANES), F32),
            pltpu.VMEM((BASES * CHUNK, LANES), F32),
        ],
        12_000_000_000,
    )(live, near, left, right, mix)


def final_call(feat, pos, msg, received, gain, up, down, long_proj, again, aup, adown):
    return call(final_body, "final", (ATOMS, LANES), [whole()] * 11, [], 2_400_000_000)(
        feat, pos, msg, received, gain, up, down, long_proj, again, aup, adown
    )


def passed_along(array, axis, by):
    count = lax.axis_size(axis)
    return lax.ppermute(array, axis, [(i, (i + by) % count) for i in range(count)])


def on_device(
    features,
    positions,
    tile_lists,
    value_proj,
    radial_mix,
    charge_proj,
    screening,
    smearing,
    mesh_gain,
    mesh_up,
    mesh_down,
    long_proj,
    atom_gain,
    atom_up,
    atom_down,
):
    feat, pos = features[0, 0], positions[0, 0]
    everyone = ("wide", "sixteen")
    spread = spread_call(feat, pos, charge_proj)
    packed = pack_call(feat, pos, value_proj)
    below = passed_along(packed, "sixteen", 1)
    above = passed_along(packed, "sixteen", -1)
    near = jnp.concatenate([below, packed, above], axis=0)
    left = passed_along(near, "wide", 1)
    right = passed_along(near, "wide", -1)
    received = lax.all_to_all(spread, everyone, split_axis=0, concat_axis=0, tiled=True)
    filtered = filter_call(screening, smearing, received)
    returned = lax.all_to_all(filtered, everyone, split_axis=0, concat_axis=0, tiled=True)
    codes = jnp.arange(36, dtype=jnp.int32)
    live = jnp.any(tile_lists[0, 0][:, :, None] == codes, axis=1).astype(jnp.int32)
    messages = short_call(live, near, left, right, radial_mix)
    updated = final_call(
        feat,
        pos,
        messages,
        returned,
        mesh_gain[None],
        mesh_up,
        mesh_down,
        long_proj,
        atom_gain[None],
        atom_up,
        atom_down,
    )
    return updated[None, None]


def solution(mesh):
    block = P("wide", "sixteen", None, None)
    channel = P(("wide", "sixteen"))
    in_specs = (block,) * 3 + (P(),) * 3 + (channel,) * 2 + (P(),) * 7
    return jax.shard_map(
        on_device, mesh=mesh, in_specs=in_specs, out_specs=block, check_vma=False
    )
```

```python
import functools
import math

import jax
import jax.numpy as jnp
import ml_dtypes
import numpy as np
from jax import lax
from jax.experimental import pallas as pl
from jax.experimental.pallas import tpu as pltpu
from jax.sharding import PartitionSpec as P

F32 = jnp.float32
BF = jnp.bfloat16
MESH = 64
LANES = 128
ATOMS = 512
CHUNK = 64
CHUNKS = ATOMS // CHUNK
BASES = 16
ROWS = 24
PACK = 528
FAR = 1000.0
CUTOFF = 0.05
MID = 8
LIMIT = 32 * 1024 * 1024
SHORT_COST = 12_000_000_000
PREPARE_COST = 1_000


def split(x):
    hi = x.astype(BF)
    return hi, (x - hi.astype(F32)).astype(BF)


def dot(a, b):
    return jnp.dot(a, b, preferred_element_type=F32)


def dot_nt(a, b):
    return lax.dot_general(a, b, (((1,), (1,)), ((), ())), preferred_element_type=F32)


def dot3(a, b):
    ah, al = split(a)
    bh, bl = split(b)
    return dot(ah, bh) + (dot(ah, bl) + dot(al, bh))


def rows_of(pos_ref):
    return jnp.concatenate([pos_ref[0], pos_ref[1], pos_ref[2]], axis=0)


def lane_iota(shape):
    return lax.broadcasted_iota(jnp.int32, shape, len(shape) - 1)


def half_turn(x):
    return pltpu.roll(x, 64, x.ndim - 1)


def pack_body(feat_a, pos_a, feat_b, pos_b, feat_c, pos_c, proj_ref, out_ref):
    proj = proj_ref[...]
    for k, (feat, pos_ref) in enumerate(((feat_a, pos_a), (feat_b, pos_b), (feat_c, pos_c))):
        base = k * PACK
        out_ref[base : base + ATOMS, :] = dot3(feat[...], proj)
        for d in range(3):
            pos = pos_ref[d]
            for t in range(4):
                row = base + ATOMS + 4 * d + t
                out_ref[row : row + 1, :] = pos[:, t * LANES : (t + 1) * LANES]
        out_ref[base + ATOMS + 12 : base + PACK, :] = jnp.zeros((PACK - ATOMS - 12, LANES), F32)


def hat(distance):
    return jnp.maximum(1.0 - jnp.abs(distance), 0.0)


def planes_of(uy, uz, half, z, low):
    depth = jnp.abs(uz - z)
    hz = hat(jnp.minimum(depth, 64.0 - depth))
    top = jnp.where(low, hat(uy - 4.0) * hz, 0.0)
    return [hat(uy - half) * hz, hat(uy - 2.0 - half) * hz, top]


def planes_across(pos):
    filled = jnp.concatenate([pos, jnp.zeros((5, ATOMS), F32)], axis=0)
    columns = filled.T
    wide = lambda d, scale: jnp.broadcast_to(columns[:, d : d + 1] * scale, (ATOMS, LANES))
    lane = lane_iota((1, LANES))
    half, z = (lane // 64).astype(F32), (lane % 64).astype(F32)
    return jnp.concatenate(planes_of(wide(1, 4.0), wide(2, float(MESH)), half, z, lane < 64), axis=1)


def planes_down(pos):
    row = lax.broadcasted_iota(jnp.int32, (LANES, 1), 0)
    half, z = (row // 64).astype(F32), (row % 64).astype(F32)
    uy, uz = pos[1:2, :] * 4.0, pos[2:3, :] * float(MESH)
    return jnp.concatenate(planes_of(uy, uz, half, z, row < 64), axis=0)


def spread_body(feat_ref, pos_ref, proj_ref, out_ref):
    pos = rows_of(pos_ref)
    wh, wl = split(planes_across(pos))
    ux = pos[0:1, :] * 8.0
    charges = dot3(feat_ref[...], proj_ref[...]).T
    highs, lows = [], []
    for x in range(9):
        high, low = split(charges * hat(ux - float(x)))
        highs.append(high)
        lows.append(low)
    high = jnp.concatenate(highs, axis=0)
    low = jnp.concatenate(lows, axis=0)
    result = dot(high, wh) + (dot(low, wh) + dot(high, wl))
    piece = lambda x, k: result[x * LANES : (x + 1) * LANES, k * LANES : (k + 1) * LANES]
    edge = [half_turn(piece(8, 0)), piece(8, 0), half_turn(piece(8, 1)), piece(8, 1), half_turn(piece(8, 2))]
    below = lane_iota((1, LANES)) < 64
    for x in range(8):
        out_ref[pl.ds(x, LANES, stride=ROWS), :] = piece(x, 0)
        out_ref[pl.ds(8 + x, LANES, stride=ROWS), :] = piece(x, 1)
        top = piece(x, 2)
        out_ref[pl.ds(16 + x, LANES, stride=ROWS), :] = jnp.where(below, top, edge[x]) if x < 5 else top


def real_basis():
    n = np.arange(MESH)
    rows = []
    for k in range(MESH):
        if k == 0:
            rows.append(np.full(MESH, 1.0 / 8.0))
        elif k == MESH // 2:
            rows.append(np.where(n % 2 == 0, 1.0, -1.0) / 8.0)
        elif k < MESH // 2:
            rows.append(np.cos(2 * np.pi * (k * n % MESH) / MESH) * math.sqrt(2.0) / 8.0)
        else:
            rows.append(np.sin(2 * np.pi * ((MESH - k) * n % MESH) / MESH) * math.sqrt(2.0) / 8.0)
    return np.stack(rows)


def halves(table):
    high = table.astype(np.float32).astype(ml_dtypes.bfloat16)
    low = (table - high.astype(np.float64)).astype(np.float32).astype(ml_dtypes.bfloat16)
    return high, low


def stacked(table):
    high, low = halves(table)
    return np.concatenate([high, low, high], axis=1)


def squared(table):
    high, low = halves(table)
    top = np.concatenate([high, low], axis=1)
    bottom = np.concatenate([high, np.zeros_like(low)], axis=1)
    return np.concatenate([top, bottom], axis=0)


def filter_tables():
    q = real_basis()
    y_forward = np.concatenate([q[:, 0::2], q[:, 1::2]], axis=0)
    y_back = np.concatenate([q.T[0::2], q.T[1::2]], axis=0)
    twice = np.kron(np.eye(2), q.T)
    tables = [stacked(q), stacked(y_forward), squared(twice), squared(twice.T), stacked(y_back), stacked(q.T)]
    wide = 2 * LANES
    filled = [np.pad(t.astype(np.float32), ((0, 0), (0, wide - t.shape[1]))) for t in tables]
    return np.concatenate(filled, axis=0).astype(ml_dtypes.bfloat16)


def stack_rows(x):
    high, low = split(x)
    return jnp.concatenate([high, high, low], axis=0)


def sum_halves(x):
    return x[:, :LANES] + x[:, LANES:]


def filter_body(
    screen_ref, smear_ref, in_ref, table_ref, out_ref, turn_ref, edge_ref
):
    devices = 128
    low = lane_iota((1, LANES)) < 64
    place = lax.broadcasted_iota(jnp.int32, (devices, 1), 0) % 16

    side = [in_ref[pl.ds(16 + y, devices, stride=ROWS), :] for y in range(5)]
    corner = jnp.where(place == 0, pltpu.roll(side[4], 113, 0), pltpu.roll(side[4], 1, 0))
    side[0] = side[0] + corner
    for h in range(2):
        both = jnp.where(low, half_turn(side[2 * h]), side[2 * h + 1])
        edge_ref[h * devices : (h + 1) * devices, :] = pltpu.roll(both, 16, 0)

    first_row = lax.broadcasted_iota(jnp.int32, (8, 1), 0) == 0
    x_forward = table_ref[0:64, 0:192]
    for s in range(0, 16, 2):
        parts = []
        for k in range(4):
            d, h = s + k // 2, k % 2
            tiles = []
            for w in range(8):
                at = w * 16 + d
                tile = in_ref[at * ROWS + h * 8 : at * ROWS + h * 8 + 8, :]
                edge = edge_ref[h * devices + at : h * devices + at + 1, :]
                tile = tile + jnp.where(first_row, edge, 0.0)
                if h == 0:
                    below = (w * 16 + (d + 15) % 16) * ROWS + 16
                    tile = tile + jnp.where(low, in_ref[below : below + 8, :], 0.0)
                tiles.append(tile)
            parts.append(jnp.concatenate(tiles, axis=0))
        result = dot(x_forward, stack_rows(jnp.concatenate(parts, axis=1)))
        for k in range(4):
            turn_ref[pl.ds(2 * s + k, MESH, stride=32), :] = result[:, k * LANES : (k + 1) * LANES]

    kappa = screen_ref[0]
    kappa_sq = kappa * kappa
    decay = -0.5 * smear_ref[0] * smear_ref[0]
    lane = lane_iota((1, LANES))
    fold = lambda k: jnp.minimum(k, MESH - k).astype(F32)
    nz = fold(lane % 64)
    ny = fold(lax.broadcasted_iota(jnp.int32, (MESH, 1), 0))
    scale = 4.0 * math.pi**2
    yz = (ny * ny + nz * nz) * scale
    y_forward, z_forward = table_ref[64:192, 0:96], table_ref[192:448, :]
    z_back, y_back = table_ref[448:704, :], table_ref[704:768, 0:192]
    group = 32
    for start in range(0, 32, group):
        planes = []
        for p in range(start, start + group, 2):
            pairs = jnp.concatenate(
                [turn_ref[(2 * p + k) * 32 : (2 * p + k + 1) * 32, :] for k in range(4)], axis=1
            )
            result = dot(y_forward, stack_rows(pairs))
            for k in range(2):
                a = result[:, 2 * k * LANES : (2 * k + 1) * LANES]
                b = result[:, (2 * k + 1) * LANES : (2 * k + 2) * LANES]
                straight = jnp.where(low, a[:MESH], b[MESH:])
                planes.append(straight + half_turn(jnp.where(low, b[:MESH], a[MESH:])))
        stack = jnp.concatenate(planes, axis=0)
        stack = sum_halves(dot(jnp.concatenate(split(stack), axis=1), z_forward))
        gains = []
        for p in range(start, start + group):
            nx = fold(2 * p + lane // 64)
            square = yz + nx * nx * scale
            gains.append(kappa_sq * jnp.exp(square * decay) / (square + kappa_sq))
        stack = stack * jnp.concatenate(gains, axis=0)
        stack = sum_halves(dot(jnp.concatenate(split(stack), axis=1), z_back))
        for g in range(0, group, 4):
            pair = jnp.concatenate([stack[(g + k) * MESH : (g + k + 1) * MESH] for k in range(4)], axis=1)
            result = dot(y_back, stack_rows(pair))
            for k in range(4):
                p = start + g + k
                a = result[:32, k * LANES : (k + 1) * LANES]
                b = result[32:, k * LANES : (k + 1) * LANES]
                turn_ref[2 * p * 32 : 2 * p * 32 + 32, :] = jnp.where(low, a, half_turn(b))
                turn_ref[2 * p * 32 + 32 : 2 * p * 32 + 64, :] = jnp.where(low, half_turn(a), b)

    x_back = table_ref[768:832, 0:192]
    for s in range(0, 16, 2):
        pair = jnp.concatenate(
            [turn_ref[pl.ds(2 * s + k, MESH, stride=32), :] for k in range(4)], axis=1
        )
        result = dot(x_back, stack_rows(pair))
        for w in range(8):
            for k in range(4):
                d, h = s + k // 2, k % 2
                at = (w * 16 + d) * ROWS
                tile = result[w * 8 : (w + 1) * 8, k * LANES : (k + 1) * LANES]
                out_ref[at + h * 8 : at + h * 8 + 8, :] = tile
                if h == 0:
                    below = (w * 16 + (d + 15) % 16) * ROWS + 16
                    out_ref[below : below + 8, :] = jnp.where(low, tile, 0.0)

    ahead = [pltpu.roll(out_ref[pl.ds(8 * h, devices, stride=ROWS), :], 112, 0) for h in range(2)]
    turned = [half_turn(x) for x in ahead]
    corner = jnp.where(place == 15, pltpu.roll(turned[0], 15, 0), pltpu.roll(turned[0], 127, 0))
    for y, high in enumerate([turned[0], ahead[0], turned[1], ahead[1], corner]):
        rows = pl.ds(16 + y, devices, stride=ROWS)
        out_ref[rows, :] = jnp.where(low, out_ref[rows, :], high)


ENVELOPE = (
    0.9999999991137324,
    -0.4674010362718563,
    0.0945531128786198,
    -0.011119339660821159,
    0.0008600612678157039,
    -4.252312938118321e-05,
)


def short_body(
    blocks, units, live_ref, pos_ref, part_ref, mix_ref, *rest
):
    *packs, out_ref, val_ref, win_ref, own_ref = rest
    lane = lane_iota((1, LANES))
    filled = jnp.concatenate([rows_of(pos_ref), jnp.zeros((5, ATOMS), F32)], axis=0)
    columns = filled.T
    for d, scale in ((0, 0.125), (1, 0.0625), (2, 1.0)):
        own_ref[d * ATOMS : (d + 1) * ATOMS, :] = jnp.broadcast_to(
            columns[:, d : d + 1] * scale, (ATOMS, LANES)
        )

    row = lax.broadcasted_iota(jnp.int32, (16, 1), 0)
    axis, tile = row // 4, row % 4
    pick = lambda x, y, z: jnp.where(axis == 0, x, jnp.where(axis == 1, y, z))
    scale = pick(0.125, 0.0625, 1.0)
    wrap_low = jnp.where((axis == 2) & (tile == 0), -1.0, 0.0)
    wrap_high = jnp.where((axis == 2) & (tile == 3), 1.0, 0.0)
    for k, nb in enumerate(blocks):
        dx, dy = nb // 3 - 1, nb % 3 - 1
        ref, base = packs[0 if dx < 1 else -1], (dy + 1) * PACK
        high, low = split(ref[base : base + ATOMS, :])
        both = jnp.concatenate([high, low], axis=1)
        val_ref[k, 32 : 32 + ATOMS, :] = both
        val_ref[k, 0:32, :] = both[ATOMS - 32 :, :]
        val_ref[k, ATOMS + 32 :, :] = both[:32, :]
        pos = (ref[base + ATOMS : base + PACK, :] + pick(float(dx), float(dy), 0.0)) * scale
        up = pltpu.roll(pos, 32, 1)
        before = jnp.where(tile == 0, pltpu.roll(up, 13, 0), pltpu.roll(up, 1, 0)) + wrap_low
        win_ref[k, 0] = jnp.where(lane < 32, before, up)
        down = pltpu.roll(pos, 96, 1)
        after = jnp.where(tile == 3, pltpu.roll(down, 3, 0), pltpu.roll(down, 15, 0)) + wrap_high
        win_ref[k, 1] = jnp.where(lane < 96, down, after)

    me = lax.broadcasted_iota(jnp.int32, (CHUNK, LANES), 0) + 32
    itself = (me == lane_iota((CHUNK, LANES))).astype(F32)
    zero = jnp.zeros((LANES, LANES), BF)
    half = BASES // 2

    def chunk(acc_a, acc_b, m, carry):
        t = m // 2
        parity = m % 2
        even = parity == 0
        tile_a = jnp.where(even, (t + 3) % 4, t)
        tile_b = jnp.where(even, t, (t + 1) % 4)
        from_first = lane < jnp.where(even, 32, 96)
        start = pl.multiple_of(m * CHUNK, CHUNK)

        for k, nb in enumerate(blocks):
            live_a = live_ref[t, nb * 4 + tile_a]
            live_b = live_ref[t, nb * 4 + tile_b]

            @pl.when(live_a + live_b > 0)
            def _(k=k, nb=nb, live_a=live_a, live_b=live_b):
                values = val_ref[k, pl.ds(start, LANES), :]
                rhs = jnp.concatenate(
                    [values, jnp.concatenate([values[:, :LANES], zero], axis=1)], axis=0
                )
                for unit in range(2):
                    pltpu.matmul_push_rhs(rhs, 0, unit)
                far_a = (1 - live_a).astype(F32) * FAR
                far_b = (1 - live_b).astype(F32) * FAR
                take = lambda d: win_ref[k, parity, pl.ds(4 * d + t, 1), :]
                xj = take(0) + jnp.where(from_first, far_a, far_b)
                dx = xj - own_ref[pl.ds(start, CHUNK), :]
                dy = take(1) - own_ref[pl.ds(ATOMS + start, CHUNK), :]
                dz = take(2) - own_ref[pl.ds(2 * ATOMS + start, CHUNK), :]
                s = (dx * dx + dy * dy + dz * dz) * (1.0 / CUTOFF**2)
                if nb == 4:
                    s = jnp.maximum(s, itself)
                s = jnp.minimum(s, 1.0)
                q = s * lax.rsqrt(jnp.maximum(s, 1e-30))
                v = q * float(BASES - 1) - float(MID)
                env = jnp.full_like(s, ENVELOPE[-1])
                for c in ENVELOPE[-2::-1]:
                    env = env * s + c
                rest = 1.0 - s
                middle = jnp.exp(-0.5 * v * v) * (env * (rest * rest))
                up, down = jnp.exp(v), jnp.exp(-v)
                terms = [None] * BASES
                terms[MID] = middle
                for b in range(MID + 1, BASES):
                    terms[b] = terms[b - 1] * up
                for b in range(MID - 1, -1, -1):
                    terms[b] = terms[b + 1] * down
                sides = [jnp.concatenate(split(x), axis=1) for x in terms]
                pltpu.matmul_acc_lhs(acc_a, jnp.concatenate(sides[:half], axis=0), load_staged_rhs=0)
                pltpu.matmul_acc_lhs(acc_b, jnp.concatenate(sides[half:], axis=0), load_staged_rhs=0)

        total = part_ref[pl.ds(start, CHUNK), :]
        for unit, acc in enumerate((acc_a, acc_b)):
            found = sum_halves(pltpu.matmul_pop(acc))
            for j in range(half):
                b = unit * half + j
                weight = mix_ref[b : b + 1, :] * math.exp(-0.5 * (b - MID) ** 2)
                total = total + found[j * CHUNK : (j + 1) * CHUNK, :] * weight
        out_ref[pl.ds(start, CHUNK), :] = total
        return carry

    pl.run_scoped(
        lambda acc_a, acc_b: lax.fori_loop(0, CHUNKS, functools.partial(chunk, acc_a, acc_b), 0), *units
    )


def silu(v):
    half = 0.5 * v
    return half + half * jnp.tanh(half)


def stack_lanes(x):
    high, low = split(x)
    return jnp.concatenate([high, low, high], axis=1)


def beside(x):
    return jnp.concatenate(split(x), axis=1)


def prepare_body(pos_ref, gain_ref, up_ref, down_ref, long_ref, again_ref, aup_ref, adown_ref, out_ref, hat_out):
    out_ref[0:256, 0:384] = stack_lanes(up_ref[...].T * gain_ref[...])
    down = stack_lanes(down_ref[...].T)
    out_ref[256:384, :] = down[:, :512]
    out_ref[384:512, 0:256] = down[:, 512:]
    out_ref[1536:1664, :] = beside((aup_ref[...].T * again_ref[...]).T)
    out_ref[1664:1920, 0:256] = beside(adown_ref[...])
    out_ref[384:512, 256:512] = beside(long_ref[...])
    pos = rows_of(pos_ref)
    high, low = split(planes_down(pos))
    main = 2 * LANES
    pieces = [high[:main], high[:main], low[:main], high[main : main + 64], high[main : main + 64], low[main:]]
    out_ref[512:1536, :] = jnp.concatenate(pieces, axis=0)
    ux = pos[0:1, :] * 8.0
    hats = [hat(ux - float(x)) for x in range(9)] + [jnp.zeros((7, ATOMS), F32)]
    hat_out[...] = jnp.concatenate(hats, axis=0)


def dot_beside(x, pair):
    high, low = split(x)
    width = pair.shape[1] // 2
    wide = dot(high, pair)
    return wide[:, :width] + (wide[:, width:] + dot(low, pair[:, :width]))


def final_body(msg_ref, in_ref, set_ref, hat_ref, out_ref):
    up = set_ref[0:256, 0:384]
    down = jnp.concatenate([set_ref[256:384, :], set_ref[384:512, 0:256]], axis=1)
    mesh_out = []
    width = 12
    for r in range(0, ROWS, width):
        cells = jnp.concatenate(
            [in_ref[pl.ds(r + k, LANES, stride=ROWS), :] for k in range(width)], axis=1
        )
        inverse = lax.rsqrt(jnp.mean(cells * cells, axis=0, keepdims=True) + 1e-06)
        hidden = silu(dot(up, stack_rows(cells * inverse)))
        result = dot(down, stack_rows(hidden))
        mesh_out += [result[:, k * LANES : (k + 1) * LANES] for k in range(width)]
    below = lane_iota((1, LANES)) < 64
    top = mesh_out[16:]
    mixed = lambda a, b: jnp.where(below, half_turn(a), b)
    edge = [mixed(top[0], top[1]), mixed(top[2], top[3]), half_turn(top[4])]
    stacks = []
    for x in range(9):
        first, second, last = edge if x == 8 else [mesh_out[x], mesh_out[8 + x], top[x]]
        high, low = split(jnp.concatenate([first, second], axis=1))
        rounded = last.astype(BF).astype(F32)
        both = jnp.where(below, rounded, half_turn(last - rounded))
        stacks.append(jnp.concatenate([high, low, high, both.astype(BF), rounded.astype(BF)], axis=1))
    found = dot(jnp.concatenate(stacks, axis=0), set_ref[512:1536, :])
    total = None
    for x in range(9):
        term = found[x * LANES : (x + 1) * LANES] * hat_ref[x : x + 1, :]
        total = term if total is None else total + term
    summed = msg_ref[...] + dot_beside(total.T, set_ref[384:512, 256:512])
    inverse = lax.rsqrt(jnp.mean(summed * summed, axis=1, keepdims=True) + 1e-06)
    hidden = silu(dot_beside(summed * inverse, set_ref[1536:1664, :]))
    out_ref[...] = summed + dot_beside(hidden, set_ref[1664:1920, 0:256])


def whole():
    return pl.BlockSpec(memory_space=pltpu.VMEM)


def scalars():
    return pl.BlockSpec(memory_space=pltpu.SMEM)


def in_hbm(x):
    return pltpu.with_memory_space_constraint(x, pltpu.HBM)


def remote():
    return pl.BlockSpec(memory_space=pltpu.HBM)


class Fetched:
    def __init__(self, source, target, semaphore, first, cuts):
        self.target = target
        self.copies = []
        for k, (low, high) in enumerate(zip(cuts[:-1], cuts[1:])):
            rows = pl.ds(low, high - low)
            copy = pltpu.make_async_copy(source.at[rows], target.at[rows], semaphore.at[first + k])
            copy.start()
            self.copies.append([low, high, copy])

    def __getitem__(self, index):
        rows = index[0] if isinstance(index, tuple) else index
        if isinstance(rows, slice):
            start, stop = rows.start or 0, self.target.shape[0] if rows.stop is None else rows.stop
        elif isinstance(rows, int):
            start, stop = rows, rows + 1
        else:
            start, stop = 0, self.target.shape[0]
        for entry in self.copies:
            if entry[2] is not None and entry[0] < stop and entry[1] > start:
                entry[2].wait()
                entry[2] = None
        return self.target[index]


def call(body, name, shapes, places, scratch, cost, operands, cuts={}):
    specs = {"v": whole, "s": scalars, "h": remote}
    far = [i for i, p in enumerate(places) if p == "h"]
    buffers = [pltpu.VMEM(operands[i].shape, operands[i].dtype) for i in far]
    count = len(places)
    parts = [cuts.get(i, (0, operands[i].shape[0])) for i in far]
    firsts = [sum(len(p) - 1 for p in parts[:k]) for k in range(len(far) + 1)]

    def kernel(*refs):
        inputs, rest = list(refs[:count]), refs[count:]
        if far:
            held, semaphores = rest[-len(far) - 1 : -1], rest[-1]
            for k, i in enumerate(far):
                inputs[i] = Fetched(inputs[i], held[k], semaphores, firsts[k], parts[k])
            rest = rest[: -len(far) - 1]
        body(*inputs, *rest)

    extra = buffers + [pltpu.SemaphoreType.DMA((firsts[-1],))] if far else []
    return pl.pallas_call(
        kernel,
        out_shape=[jax.ShapeDtypeStruct(x, F32) if isinstance(x, tuple) else x for x in shapes],
        in_specs=[specs[p]() for p in places],
        out_specs=[whole()] * len(shapes),
        scratch_shapes=list(scratch) + extra,
        name=name,
        compiler_params=pltpu.CompilerParams(vmem_limit_bytes=LIMIT),
        cost_estimate=pl.CostEstimate(flops=cost, bytes_accessed=4 * 1024 * 1024, transcendentals=0),
    )(*operands)


def pack_call(*operands):
    return call(pack_body, "pack", [(3 * PACK, LANES)], "vvvvvvv", [], 12_000_000_000, operands)[0]


def spread_call(feat, pos, proj):
    operands = [in_hbm(x) for x in (feat, pos, proj)]
    return call(spread_body, "spread", [(LANES * ROWS, LANES)], "hhh", [], 1_200_000_000, operands)[0]


def prepare_call(*operands):
    shapes = [jax.ShapeDtypeStruct((1920, 512), BF), (16, ATOMS)]
    return call(prepare_body, "prepare", shapes, "v" * 8, [], PREPARE_COST, operands)


def filter_call(screening, smearing, received):
    scratch = [pltpu.VMEM((MESH * 32, LANES), F32), pltpu.VMEM((256, LANES), F32)]
    operands = (screening, smearing, received, in_hbm(jnp.asarray(filter_tables())))
    shapes = [(LANES * ROWS, LANES)]
    cuts = {3: (0, 64, 832)}
    return call(filter_body, "filter", shapes, "ssvh", scratch, 2_000_000_000, operands, cuts)[0]


def short_call(mesh, blocks, *operands):
    with jax.sharding.use_abstract_mesh(mesh.abstract_mesh):
        units = [pltpu.ACC(i)((BASES // 2 * CHUNK, 2 * LANES), F32) for i in range(2)]
    scratch = [
        pltpu.VMEM((len(blocks), ATOMS + 64, 2 * LANES), BF),
        pltpu.VMEM((len(blocks), 2, 16, LANES), F32),
        pltpu.VMEM((3 * ATOMS, LANES), F32),
    ]
    body = functools.partial(short_body, blocks, units)
    places = "s" + "v" * (len(operands) - 1)
    return call(body, "short_range", [(ATOMS, LANES)], places, scratch, SHORT_COST, operands)[0]


def final_call(messages, returned, weights, hats):
    operands = (messages, returned, in_hbm(weights), in_hbm(hats))
    cuts = {2: (0, 512, 1536, 1920)}
    return call(final_body, "final", [(ATOMS, LANES)], "vvhh", [], 2_400_000_000, operands, cuts)[0]


def passed_along(array, axis, by):
    count = lax.axis_size(axis)
    return lax.ppermute(array, axis, [(i, (i + by) % count) for i in range(count)])


def on_device(
    mesh,
    features,
    positions,
    tile_lists,
    value_proj,
    radial_mix,
    charge_proj,
    screening,
    smearing,
    mesh_gain,
    mesh_up,
    mesh_down,
    long_proj,
    atom_gain,
    atom_up,
    atom_down,
):
    feat, pos = features[0, 0], positions.reshape(3, 1, ATOMS)
    everyone = ("wide", "sixteen")
    feat_below = passed_along(feat, "sixteen", 1)
    feat_above = passed_along(feat, "sixteen", -1)
    pos_below = passed_along(pos, "sixteen", 1)
    pos_above = passed_along(pos, "sixteen", -1)
    spread = spread_call(feat, pos, charge_proj)
    received = lax.all_to_all(spread, everyone, split_axis=0, concat_axis=0, tiled=True)
    near = pack_call(feat_below, pos_below, feat, pos, feat_above, pos_above, value_proj)
    left = passed_along(near, "wide", 1)
    right = passed_along(near, "wide", -1)
    codes = jnp.arange(36, dtype=jnp.int32)
    live = jnp.any(tile_lists[0, 0][:, :, None] == codes, axis=1).astype(jnp.int32)
    prepared = prepare_call(
        pos, mesh_gain[None], mesh_up, mesh_down, long_proj, atom_gain[None], atom_up, atom_down
    )
    part = short_call(mesh, (3, 4, 5), live, pos, feat, radial_mix, near)
    received, part = lax.optimization_barrier((received, part))
    filtered = filter_call(screening, smearing, received)
    returned = lax.all_to_all(filtered, everyone, split_axis=0, concat_axis=0, tiled=True)
    messages = short_call(mesh, (0, 1, 2, 6, 7, 8), live, pos, part, radial_mix, left, right)
    updated = final_call(messages, returned, *prepared)
    return updated[None, None]


def solution(mesh):
    block = P("wide", "sixteen", None, None)
    channel = P(("wide", "sixteen"))
    in_specs = (block,) * 3 + (P(),) * 3 + (channel,) * 2 + (P(),) * 7
    return jax.shard_map(
        functools.partial(on_device, mesh), mesh=mesh, in_specs=in_specs, out_specs=block, check_vma=False
    )
```

```python
import functools
import math

import jax
import jax.numpy as jnp
import ml_dtypes
import numpy as np
from jax import lax
from jax.experimental import pallas as pl
from jax.experimental.pallas import tpu as pltpu
from jax.sharding import PartitionSpec as P

F32 = jnp.float32
BF = jnp.bfloat16
MESH = 64
LANES = 128
ATOMS = 512
CHUNK = 64
CHUNKS = ATOMS // CHUNK
BASES = 16
ROWS = 24
PACK = 528
TURN = 40
FAR = 1000.0
CUTOFF = 0.05
MID = 8
LIMIT = 32 * 1024 * 1024
SHORT_COST = 12_000_000_000
PACK_COST = 50_000_000
PREPARE_COST = 1_000


def split(x):
    hi = x.astype(BF)
    return hi, (x - hi.astype(F32)).astype(BF)


def dot(a, b):
    return jnp.dot(a, b, preferred_element_type=F32)


def dot_nt(a, b):
    return lax.dot_general(a, b, (((1,), (1,)), ((), ())), preferred_element_type=F32)


def dot3(a, b):
    ah, al = split(a)
    bh, bl = split(b)
    return dot(ah, bh) + (dot(ah, bl) + dot(al, bh))


def rows_of(pos_ref):
    return jnp.concatenate([pos_ref[0], pos_ref[1], pos_ref[2]], axis=0)


def lane_iota(shape):
    return lax.broadcasted_iota(jnp.int32, shape, len(shape) - 1)


def half_turn(x):
    return pltpu.roll(x, 64, x.ndim - 1)


def pack_body(feat_ref, pos_ref, proj_ref, out_ref):
    for d in range(3):
        pos = pos_ref[d]
        for t in range(4):
            row = ATOMS + 4 * d + t
            out_ref[row : row + 1, :] = pos[:, t * LANES : (t + 1) * LANES]
    out_ref[ATOMS + 12 : PACK, :] = jnp.zeros((PACK - ATOMS - 12, LANES), F32)
    out_ref[0:ATOMS, :] = dot3(feat_ref[...], proj_ref[...])


def hat(distance):
    return jnp.maximum(1.0 - jnp.abs(distance), 0.0)


def planes_of(uy, uz, half, z, low):
    depth = jnp.abs(uz - z)
    hz = hat(jnp.minimum(depth, 64.0 - depth))
    top = jnp.where(low, hat(uy - 4.0) * hz, 0.0)
    return [hat(uy - half) * hz, hat(uy - 2.0 - half) * hz, top]


def planes_across(pos):
    filled = jnp.concatenate([pos, jnp.zeros((5, ATOMS), F32)], axis=0)
    columns = filled.T
    wide = lambda d, scale: jnp.broadcast_to(columns[:, d : d + 1] * scale, (ATOMS, LANES))
    lane = lane_iota((1, LANES))
    half, z = (lane // 64).astype(F32), (lane % 64).astype(F32)
    return jnp.concatenate(planes_of(wide(1, 4.0), wide(2, float(MESH)), half, z, lane < 64), axis=1)


def planes_down(pos):
    row = lax.broadcasted_iota(jnp.int32, (LANES, 1), 0)
    half, z = (row // 64).astype(F32), (row % 64).astype(F32)
    uy, uz = pos[1:2, :] * 4.0, pos[2:3, :] * float(MESH)
    return jnp.concatenate(planes_of(uy, uz, half, z, row < 64), axis=0)


def spread_body(feat_ref, pos_ref, proj_ref, value_ref, pack_ref, out_ref):
    pos = rows_of(pos_ref)
    wh, wl = split(planes_across(pos))
    ux = pos[0:1, :] * 8.0
    charges = dot3(feat_ref[...], proj_ref[...]).T
    pack_body(feat_ref, pos_ref, value_ref, pack_ref)
    highs, lows = [], []
    for x in range(9):
        high, low = split(charges * hat(ux - float(x)))
        highs.append(high)
        lows.append(low)
    high = jnp.concatenate(highs, axis=0)
    low = jnp.concatenate(lows, axis=0)
    both = jnp.concatenate([wh[:, 256:320], wl[:, 256:320]], axis=1)
    wide = dot(high, jnp.concatenate([wh[:, :256], wl[:, :256], both], axis=1))
    last = wide[:, 512:]
    result = jnp.concatenate([wide[:, :256] + wide[:, 256:512], last + half_turn(last)], axis=1) + dot(low, wh)
    piece = lambda x, k: result[x * LANES : (x + 1) * LANES, k * LANES : (k + 1) * LANES]
    edge = [half_turn(piece(8, 0)), piece(8, 0), half_turn(piece(8, 1)), piece(8, 1), half_turn(piece(8, 2))]
    below = lane_iota((1, LANES)) < 64
    for x in range(8):
        out_ref[pl.ds(x, LANES, stride=ROWS), :] = piece(x, 0)
        out_ref[pl.ds(8 + x, LANES, stride=ROWS), :] = piece(x, 1)
        top = piece(x, 2)
        out_ref[pl.ds(16 + x, LANES, stride=ROWS), :] = jnp.where(below, top, edge[x]) if x < 5 else top


def real_basis():
    n = np.arange(MESH)
    rows = []
    for k in range(MESH):
        if k == 0:
            rows.append(np.full(MESH, 1.0 / 8.0))
        elif k == MESH // 2:
            rows.append(np.where(n % 2 == 0, 1.0, -1.0) / 8.0)
        elif k < MESH // 2:
            rows.append(np.cos(2 * np.pi * (k * n % MESH) / MESH) * math.sqrt(2.0) / 8.0)
        else:
            rows.append(np.sin(2 * np.pi * ((MESH - k) * n % MESH) / MESH) * math.sqrt(2.0) / 8.0)
    return np.stack(rows)


def halves(table):
    high = table.astype(np.float32).astype(ml_dtypes.bfloat16)
    low = (table - high.astype(np.float64)).astype(np.float32).astype(ml_dtypes.bfloat16)
    return high, low


def stacked(table):
    high, low = halves(table)
    return np.concatenate([high, low, high], axis=1)


def squared(table):
    high, low = halves(table)
    top = np.concatenate([high, low], axis=1)
    bottom = np.concatenate([high, np.zeros_like(low)], axis=1)
    return np.concatenate([top, bottom], axis=0)


def filter_tables():
    q = real_basis()
    y_forward = np.concatenate([q[:, 0::2], q[:, 1::2]], axis=0)
    y_back = np.concatenate([q.T[0::2], q.T[1::2]], axis=0)
    twice = np.kron(np.eye(2), q.T)
    tables = [stacked(q), stacked(y_forward), squared(twice), squared(twice.T), stacked(y_back), stacked(q.T)]
    wide = 2 * LANES
    filled = [np.pad(t.astype(np.float32), ((0, 0), (0, wide - t.shape[1]))) for t in tables]
    return np.concatenate(filled, axis=0).astype(ml_dtypes.bfloat16)


def stack_rows(x):
    high, low = split(x)
    return jnp.concatenate([high, high, low], axis=0)


def sum_halves(x):
    return x[:, :LANES] + x[:, LANES:]


def filter_body(
    screen_ref, smear_ref, in_ref, table_ref, out_ref, turn_ref, edge_ref
):
    devices = 128
    low = lane_iota((1, LANES)) < 64
    place = lax.broadcasted_iota(jnp.int32, (devices, 1), 0) % 16

    side = [in_ref[pl.ds(16 + y, devices, stride=ROWS), :] for y in range(5)]
    corner = jnp.where(place == 0, pltpu.roll(side[4], 113, 0), pltpu.roll(side[4], 1, 0))
    side[0] = side[0] + corner
    for h in range(2):
        both = jnp.where(low, half_turn(side[2 * h]), side[2 * h + 1])
        edge_ref[h * devices : (h + 1) * devices, :] = pltpu.roll(both, 16, 0)

    first_row = lax.broadcasted_iota(jnp.int32, (8, 1), 0) == 0
    stacks = []
    for s in range(0, 16, 2):
        parts = []
        for k in range(4):
            d, h = s + k // 2, k % 2
            tiles = []
            for w in range(8):
                at = w * 16 + d
                tile = in_ref[at * ROWS + h * 8 : at * ROWS + h * 8 + 8, :]
                edge = edge_ref[h * devices + at : h * devices + at + 1, :]
                tile = tile + jnp.where(first_row, edge, 0.0)
                if h == 0:
                    below = (w * 16 + (d + 15) % 16) * ROWS + 16
                    tile = tile + jnp.where(low, in_ref[below : below + 8, :], 0.0)
                tiles.append(tile)
            parts.append(jnp.concatenate(tiles, axis=0))
        stacks.append(stack_rows(jnp.concatenate(parts, axis=1)))
    x_forward = table_ref[0:64, 0:192]
    for s, stack in zip(range(0, 16, 2), stacks):
        result = dot(x_forward, stack)
        for k in range(4):
            turn_ref[pl.ds(2 * s + k, MESH, stride=TURN), :] = result[:, k * LANES : (k + 1) * LANES]

    kappa = screen_ref[0]
    kappa_sq = kappa * kappa
    decay = -0.5 * smear_ref[0] * smear_ref[0]
    lane = lane_iota((1, LANES))
    fold = lambda k: jnp.minimum(k, MESH - k).astype(F32)
    nz = fold(lane % 64)
    ny = fold(lax.broadcasted_iota(jnp.int32, (MESH, 1), 0))
    scale = 4.0 * math.pi**2
    yz = (ny * ny + nz * nz) * scale
    y_forward, z_forward = table_ref[64:192, 0:96], table_ref[192:448, :]
    z_back, y_back = table_ref[448:704, :], table_ref[704:768, 0:192]
    group = 32
    for start in range(0, 32, group):
        planes = []
        for p in range(start, start + group, 2):
            pairs = jnp.concatenate(
                [turn_ref[(2 * p + k) * TURN : (2 * p + k) * TURN + 32, :] for k in range(4)], axis=1
            )
            result = dot(y_forward, stack_rows(pairs))
            for k in range(2):
                a = result[:, 2 * k * LANES : (2 * k + 1) * LANES]
                b = result[:, (2 * k + 1) * LANES : (2 * k + 2) * LANES]
                straight = jnp.where(low, a[:MESH], b[MESH:])
                planes.append(straight + half_turn(jnp.where(low, b[:MESH], a[MESH:])))
        stack = jnp.concatenate(planes, axis=0)
        stack = sum_halves(dot(jnp.concatenate(split(stack), axis=1), z_forward))
        gains = []
        for p in range(start, start + group):
            nx = fold(2 * p + lane // 64)
            square = yz + nx * nx * scale
            gains.append(kappa_sq * jnp.exp(square * decay) / (square + kappa_sq))
        stack = stack * jnp.concatenate(gains, axis=0)
        stack = sum_halves(dot(jnp.concatenate(split(stack), axis=1), z_back))
        for g in range(0, group, 4):
            pair = jnp.concatenate([stack[(g + k) * MESH : (g + k + 1) * MESH] for k in range(4)], axis=1)
            result = dot(y_back, stack_rows(pair))
            for k in range(4):
                p = start + g + k
                a = result[:32, k * LANES : (k + 1) * LANES]
                b = result[32:, k * LANES : (k + 1) * LANES]
                turn_ref[2 * p * TURN : 2 * p * TURN + 32, :] = jnp.where(low, a, half_turn(b))
                turn_ref[(2 * p + 1) * TURN : (2 * p + 1) * TURN + 32, :] = jnp.where(low, half_turn(a), b)

    x_back = table_ref[768:832, 0:192]
    for s in range(0, 16, 2):
        pair = jnp.concatenate(
            [turn_ref[pl.ds(2 * s + k, MESH, stride=TURN), :] for k in range(4)], axis=1
        )
        result = dot(x_back, stack_rows(pair))
        for w in range(8):
            for k in range(4):
                d, h = s + k // 2, k % 2
                at = (w * 16 + d) * ROWS
                tile = result[w * 8 : (w + 1) * 8, k * LANES : (k + 1) * LANES]
                out_ref[at + h * 8 : at + h * 8 + 8, :] = tile
                if h == 0:
                    below = (w * 16 + (d + 15) % 16) * ROWS + 16
                    out_ref[below : below + 8, :] = jnp.where(low, tile, 0.0)

    ahead = [pltpu.roll(out_ref[pl.ds(8 * h, devices, stride=ROWS), :], 112, 0) for h in range(2)]
    turned = [half_turn(x) for x in ahead]
    corner = jnp.where(place == 15, pltpu.roll(turned[0], 15, 0), pltpu.roll(turned[0], 127, 0))
    for y, high in enumerate([turned[0], ahead[0], turned[1], ahead[1], corner]):
        rows = pl.ds(16 + y, devices, stride=ROWS)
        out_ref[rows, :] = jnp.where(low, out_ref[rows, :], high)


ENVELOPE = (
    0.9999999991137324,
    -0.4674010362718563,
    0.0945531128786198,
    -0.011119339660821159,
    0.0008600612678157039,
    -4.252312938118321e-05,
)


def short_body(
    blocks, units, live_ref, pos_ref, part_ref, mix_ref, *rest
):
    *packs, out_ref, val_ref, win_ref, own_ref = rest
    lane = lane_iota((1, LANES))
    filled = jnp.concatenate([rows_of(pos_ref), jnp.zeros((5, ATOMS), F32)], axis=0)
    columns = filled.T
    for d, scale in ((0, 0.125), (1, 0.0625), (2, 1.0)):
        own_ref[d * ATOMS : (d + 1) * ATOMS, :] = jnp.broadcast_to(
            columns[:, d : d + 1] * scale, (ATOMS, LANES)
        )

    row = lax.broadcasted_iota(jnp.int32, (16, 1), 0)
    axis, tile = row // 4, row % 4
    pick = lambda x, y, z: jnp.where(axis == 0, x, jnp.where(axis == 1, y, z))
    scale = pick(0.125, 0.0625, 1.0)
    wrap_low = jnp.where((axis == 2) & (tile == 0), -1.0, 0.0)
    wrap_high = jnp.where((axis == 2) & (tile == 3), 1.0, 0.0)
    for k, nb in enumerate(blocks):
        dx, dy = nb // 3 - 1, nb % 3 - 1
        ref, base = packs[0 if dx < 1 else -1], (dy + 1) * PACK
        high, low = split(ref[base : base + ATOMS, :])
        both = jnp.concatenate([high, low], axis=1)
        val_ref[k, 32 : 32 + ATOMS, :] = both
        val_ref[k, 0:32, :] = both[ATOMS - 32 :, :]
        val_ref[k, ATOMS + 32 :, :] = both[:32, :]
        pos = (ref[base + ATOMS : base + PACK, :] + pick(float(dx), float(dy), 0.0)) * scale
        up = pltpu.roll(pos, 32, 1)
        before = jnp.where(tile == 0, pltpu.roll(up, 13, 0), pltpu.roll(up, 1, 0)) + wrap_low
        win_ref[k, 0] = jnp.where(lane < 32, before, up)
        down = pltpu.roll(pos, 96, 1)
        after = jnp.where(tile == 3, pltpu.roll(down, 3, 0), pltpu.roll(down, 15, 0)) + wrap_high
        win_ref[k, 1] = jnp.where(lane < 96, down, after)

    me = lax.broadcasted_iota(jnp.int32, (CHUNK, LANES), 0) + 32
    itself = (me == lane_iota((CHUNK, LANES))).astype(F32)
    zero = jnp.zeros((LANES, LANES), BF)
    half = BASES // 2

    def chunk(acc_a, acc_b, m, carry):
        t = m // 2
        parity = m % 2
        even = parity == 0
        tile_a = jnp.where(even, (t + 3) % 4, t)
        tile_b = jnp.where(even, t, (t + 1) % 4)
        from_first = lane < jnp.where(even, 32, 96)
        start = pl.multiple_of(m * CHUNK, CHUNK)

        for k, nb in enumerate(blocks):
            live_a = live_ref[t, nb * 4 + tile_a]
            live_b = live_ref[t, nb * 4 + tile_b]

            @pl.when(live_a + live_b > 0)
            def _(k=k, nb=nb, live_a=live_a, live_b=live_b):
                values = val_ref[k, pl.ds(start, LANES), :]
                rhs = jnp.concatenate(
                    [values, jnp.concatenate([values[:, :LANES], zero], axis=1)], axis=0
                )
                for unit in range(2):
                    pltpu.matmul_push_rhs(rhs, 0, unit)
                far_a = (1 - live_a).astype(F32) * FAR
                far_b = (1 - live_b).astype(F32) * FAR
                take = lambda d: win_ref[k, parity, pl.ds(4 * d + t, 1), :]
                xj = take(0) + jnp.where(from_first, far_a, far_b)
                dx = xj - own_ref[pl.ds(start, CHUNK), :]
                dy = take(1) - own_ref[pl.ds(ATOMS + start, CHUNK), :]
                dz = take(2) - own_ref[pl.ds(2 * ATOMS + start, CHUNK), :]
                s = (dx * dx + dy * dy + dz * dz) * (1.0 / CUTOFF**2)
                if nb == 4:
                    s = jnp.maximum(s, itself)
                s = jnp.minimum(s, 1.0)
                q = s * lax.rsqrt(jnp.maximum(s, 1e-30))
                v = q * float(BASES - 1) - float(MID)
                env = jnp.full_like(s, ENVELOPE[-1])
                for c in ENVELOPE[-2::-1]:
                    env = env * s + c
                rest = 1.0 - s
                middle = jnp.exp(-0.5 * v * v) * (env * (rest * rest))
                up, down = jnp.exp(v), jnp.exp(-v)
                terms = [None] * BASES
                terms[MID] = middle
                for b in range(MID + 1, BASES):
                    terms[b] = terms[b - 1] * up
                for b in range(MID - 1, -1, -1):
                    terms[b] = terms[b + 1] * down
                sides = [jnp.concatenate(split(x), axis=1) for x in terms]
                pltpu.matmul_acc_lhs(acc_a, jnp.concatenate(sides[:half], axis=0), load_staged_rhs=0)
                pltpu.matmul_acc_lhs(acc_b, jnp.concatenate(sides[half:], axis=0), load_staged_rhs=0)

        total = part_ref[pl.ds(start, CHUNK), :]
        for unit, acc in enumerate((acc_a, acc_b)):
            found = sum_halves(pltpu.matmul_pop(acc))
            for j in range(half):
                b = unit * half + j
                weight = mix_ref[b : b + 1, :] * math.exp(-0.5 * (b - MID) ** 2)
                total = total + found[j * CHUNK : (j + 1) * CHUNK, :] * weight
        out_ref[pl.ds(start, CHUNK), :] = total
        return carry

    pl.run_scoped(
        lambda acc_a, acc_b: lax.fori_loop(0, CHUNKS, functools.partial(chunk, acc_a, acc_b), 0), *units
    )


def silu(v):
    half = 0.5 * v
    return half + half * jnp.tanh(half)


def stack_lanes(x):
    high, low = split(x)
    return jnp.concatenate([high, low, high], axis=1)


def beside(x):
    return jnp.concatenate(split(x), axis=1)


def prepare_body(pos_ref, gain_ref, up_ref, down_ref, long_ref, again_ref, aup_ref, adown_ref, out_ref, hat_out):
    out_ref[0:256, 0:384] = stack_lanes(up_ref[...].T * gain_ref[...])
    down = stack_lanes(down_ref[...].T)
    out_ref[256:384, :] = down[:, :512]
    out_ref[384:512, 0:256] = down[:, 512:]
    out_ref[1536:1664, :] = beside((aup_ref[...].T * again_ref[...]).T)
    out_ref[1664:1920, 0:256] = beside(adown_ref[...])
    out_ref[384:512, 256:512] = beside(long_ref[...])
    pos = rows_of(pos_ref)
    high, low = split(planes_down(pos))
    main = 2 * LANES
    pieces = [high[:main], high[:main], low[:main], high[main : main + 64], high[main : main + 64], low[main:]]
    out_ref[512:1536, :] = jnp.concatenate(pieces, axis=0)
    ux = pos[0:1, :] * 8.0
    hats = [hat(ux - float(x)) for x in range(9)] + [jnp.zeros((7, ATOMS), F32)]
    hat_out[...] = jnp.concatenate(hats, axis=0)


def dot_beside(x, pair):
    high, low = split(x)
    width = pair.shape[1] // 2
    wide = dot(high, pair)
    return wide[:, :width] + (wide[:, width:] + dot(low, pair[:, :width]))


def final_body(msg_ref, in_ref, set_ref, hat_ref, out_ref):
    mesh_out, stacks = [], []
    width = 12
    for r in range(0, ROWS, width):
        cells = jnp.concatenate(
            [in_ref[pl.ds(r + k, LANES, stride=ROWS), :] for k in range(width)], axis=1
        )
        inverse = lax.rsqrt(jnp.mean(cells * cells, axis=0, keepdims=True) + 1e-06)
        stacks.append(stack_rows(cells * inverse))
    up = set_ref[0:256, 0:384]
    down = jnp.concatenate([set_ref[256:384, :], set_ref[384:512, 0:256]], axis=1)
    for stack in stacks:
        result = dot(down, stack_rows(silu(dot(up, stack))))
        mesh_out += [result[:, k * LANES : (k + 1) * LANES] for k in range(width)]
    below = lane_iota((1, LANES)) < 64
    top = mesh_out[16:]
    mixed = lambda a, b: jnp.where(below, half_turn(a), b)
    edge = [mixed(top[0], top[1]), mixed(top[2], top[3]), half_turn(top[4])]
    stacks = []
    for x in range(9):
        first, second, last = edge if x == 8 else [mesh_out[x], mesh_out[8 + x], top[x]]
        high, low = split(jnp.concatenate([first, second], axis=1))
        rounded = last.astype(BF).astype(F32)
        both = jnp.where(below, rounded, half_turn(last - rounded))
        stacks.append(jnp.concatenate([high, low, high, both.astype(BF), rounded.astype(BF)], axis=1))
    found = dot(jnp.concatenate(stacks, axis=0), set_ref[512:1536, :])
    total = None
    for x in range(9):
        term = found[x * LANES : (x + 1) * LANES] * hat_ref[x : x + 1, :]
        total = term if total is None else total + term
    summed = msg_ref[...] + dot_beside(total.T, set_ref[384:512, 256:512])
    inverse = lax.rsqrt(jnp.mean(summed * summed, axis=1, keepdims=True) + 1e-06)
    hidden = silu(dot_beside(summed * inverse, set_ref[1536:1664, :]))
    out_ref[...] = summed + dot_beside(hidden, set_ref[1664:1920, 0:256])


def whole():
    return pl.BlockSpec(memory_space=pltpu.VMEM)


def scalars():
    return pl.BlockSpec(memory_space=pltpu.SMEM)


def in_hbm(x):
    return pltpu.with_memory_space_constraint(x, pltpu.HBM)


def remote():
    return pl.BlockSpec(memory_space=pltpu.HBM)


class Fetched:
    def __init__(self, source, target, semaphore, first, cuts):
        self.target = target
        self.copies = []
        for k, (low, high) in enumerate(zip(cuts[:-1], cuts[1:])):
            rows = pl.ds(low, high - low)
            copy = pltpu.make_async_copy(source.at[rows], target.at[rows], semaphore.at[first + k])
            copy.start()
            self.copies.append([low, high, copy])

    def __getitem__(self, index):
        rows = index[0] if isinstance(index, tuple) else index
        if isinstance(rows, slice):
            start, stop = rows.start or 0, self.target.shape[0] if rows.stop is None else rows.stop
        elif isinstance(rows, int):
            start, stop = rows, rows + 1
        else:
            start, stop = 0, self.target.shape[0]
        for entry in self.copies:
            if entry[2] is not None and entry[0] < stop and entry[1] > start:
                entry[2].wait()
                entry[2] = None
        return self.target[index]


def call(body, name, shapes, places, scratch, cost, operands, cuts={}):
    specs = {"v": whole, "s": scalars, "h": remote}
    far = [i for i, p in enumerate(places) if p == "h"]
    buffers = [pltpu.VMEM(operands[i].shape, operands[i].dtype) for i in far]
    count = len(places)
    parts = [cuts.get(i, (0, operands[i].shape[0])) for i in far]
    firsts = [sum(len(p) - 1 for p in parts[:k]) for k in range(len(far) + 1)]

    def kernel(*refs):
        inputs, rest = list(refs[:count]), refs[count:]
        if far:
            held, semaphores = rest[-len(far) - 1 : -1], rest[-1]
            for k, i in enumerate(far):
                inputs[i] = Fetched(inputs[i], held[k], semaphores, firsts[k], parts[k])
            rest = rest[: -len(far) - 1]
        body(*inputs, *rest)

    extra = buffers + [pltpu.SemaphoreType.DMA((firsts[-1],))] if far else []
    return pl.pallas_call(
        kernel,
        out_shape=[jax.ShapeDtypeStruct(x, F32) if isinstance(x, tuple) else x for x in shapes],
        in_specs=[specs[p]() for p in places],
        out_specs=[whole()] * len(shapes),
        scratch_shapes=list(scratch) + extra,
        name=name,
        compiler_params=pltpu.CompilerParams(vmem_limit_bytes=LIMIT),
        cost_estimate=pl.CostEstimate(flops=cost, bytes_accessed=4 * 1024 * 1024, transcendentals=0),
    )(*operands)


def spread_call(*operands):
    operands = [in_hbm(x) for x in operands]
    shapes = [(PACK, LANES), (LANES * ROWS, LANES)]
    return call(spread_body, "spread", shapes, "hhhh", [], 1_200_000_000, operands)


def prepare_call(*operands):
    shapes = [jax.ShapeDtypeStruct((1920, 512), BF), (16, ATOMS)]
    return call(prepare_body, "prepare", shapes, "v" * 8, [], PREPARE_COST, operands)


def filter_call(screening, smearing, received):
    scratch = [pltpu.VMEM((MESH * TURN, LANES), F32), pltpu.VMEM((256, LANES), F32)]
    operands = (screening, smearing, received, in_hbm(jnp.asarray(filter_tables())))
    shapes = [(LANES * ROWS, LANES)]
    cuts = {3: (0, 64, 832)}
    return call(filter_body, "filter", shapes, "ssvh", scratch, 2_000_000_000, operands, cuts)[0]


def short_call(mesh, blocks, *operands):
    with jax.sharding.use_abstract_mesh(mesh.abstract_mesh):
        units = [pltpu.ACC(i)((BASES // 2 * CHUNK, 2 * LANES), F32) for i in range(2)]
    scratch = [
        pltpu.VMEM((len(blocks), ATOMS + 64, 2 * LANES), BF),
        pltpu.VMEM((len(blocks), 2, 16, LANES), F32),
        pltpu.VMEM((3 * ATOMS, LANES), F32),
    ]
    body = functools.partial(short_body, blocks, units)
    places = "s" + "v" * (len(operands) - 1)
    return call(body, "short_range", [(ATOMS, LANES)], places, scratch, SHORT_COST, operands)[0]


def final_call(messages, returned, weights, hats):
    operands = (messages, returned, in_hbm(weights), in_hbm(hats))
    cuts = {2: (0, 512, 1536, 1920)}
    return call(final_body, "final", [(ATOMS, LANES)], "vvhh", [], 2_400_000_000, operands, cuts)[0]


def passed_along(array, axis, by):
    count = lax.axis_size(axis)
    return lax.ppermute(array, axis, [(i, (i + by) % count) for i in range(count)])


def on_device(
    mesh,
    features,
    positions,
    tile_lists,
    value_proj,
    radial_mix,
    charge_proj,
    screening,
    smearing,
    mesh_gain,
    mesh_up,
    mesh_down,
    long_proj,
    atom_gain,
    atom_up,
    atom_down,
):
    feat, pos = features[0, 0], positions.reshape(3, 1, ATOMS)
    everyone = ("wide", "sixteen")
    packed, spread = spread_call(feat, pos, charge_proj, value_proj)
    below = passed_along(packed, "sixteen", 1)
    above = passed_along(packed, "sixteen", -1)
    received = lax.all_to_all(spread, everyone, split_axis=0, concat_axis=0, tiled=True)
    near = jnp.concatenate([below, packed, above], axis=0)
    left = passed_along(near, "wide", 1)
    right = passed_along(near, "wide", -1)
    codes = jnp.arange(36, dtype=jnp.int32)
    live = jnp.any(tile_lists[0, 0][:, :, None] == codes, axis=1).astype(jnp.int32)
    prepared = prepare_call(
        pos, mesh_gain[None], mesh_up, mesh_down, long_proj, atom_gain[None], atom_up, atom_down
    )
    part = short_call(mesh, (3, 4, 5), live, pos, feat, radial_mix, near)
    received, part = lax.optimization_barrier((received, part))
    filtered = filter_call(screening, smearing, received)
    returned = lax.all_to_all(filtered, everyone, split_axis=0, concat_axis=0, tiled=True)
    messages = short_call(mesh, (0, 1, 2, 6, 7, 8), live, pos, part, radial_mix, left, right)
    updated = final_call(messages, returned, *prepared)
    return updated[None, None]


def solution(mesh):
    block = P("wide", "sixteen", None, None)
    channel = P(("wide", "sixteen"))
    in_specs = (block,) * 3 + (P(),) * 3 + (channel,) * 2 + (P(),) * 7
    return jax.shard_map(
        functools.partial(on_device, mesh), mesh=mesh, in_specs=in_specs, out_specs=block, check_vma=False
    )
```

```python
import functools
import math

import jax
import jax.numpy as jnp
import ml_dtypes
import numpy as np
from jax import lax
from jax.experimental import pallas as pl
from jax.experimental.pallas import tpu as pltpu
from jax.sharding import PartitionSpec as P

F32 = jnp.float32
BF = jnp.bfloat16
MESH = 64
LANES = 128
ATOMS = 512
CHUNK = 64
CHUNKS = ATOMS // CHUNK
BASES = 16
ROWS = 24
PACK = 528
TURN = 40
FAR = 1000.0
CUTOFF = 0.05
MID = 8
LIMIT = 32 * 1024 * 1024
SHORT_COST = 12_000_000_000
PACK_COST = 50_000_000
PREPARE_COST = 1_000


def split(x):
    hi = x.astype(BF)
    return hi, (x - hi.astype(F32)).astype(BF)


def dot(a, b):
    return jnp.dot(a, b, preferred_element_type=F32)


def dot_nt(a, b):
    return lax.dot_general(a, b, (((1,), (1,)), ((), ())), preferred_element_type=F32)


def dot3(a, b):
    ah, al = split(a)
    bh, bl = split(b)
    return dot(ah, bh) + (dot(ah, bl) + dot(al, bh))


def rows_of(pos_ref):
    return jnp.concatenate([pos_ref[0], pos_ref[1], pos_ref[2]], axis=0)


def lane_iota(shape):
    return lax.broadcasted_iota(jnp.int32, shape, len(shape) - 1)


def half_turn(x):
    return pltpu.roll(x, 64, x.ndim - 1)


def pack_body(feat_ref, pos_ref, proj_ref, out_ref):
    for d in range(3):
        pos = pos_ref[d]
        for t in range(4):
            row = ATOMS + 4 * d + t
            out_ref[row : row + 1, :] = pos[:, t * LANES : (t + 1) * LANES]
    out_ref[ATOMS + 12 : PACK, :] = jnp.zeros((PACK - ATOMS - 12, LANES), F32)
    out_ref[0:ATOMS, :] = dot3(feat_ref[...], proj_ref[...])


def hat(distance):
    return jnp.maximum(1.0 - jnp.abs(distance), 0.0)


def planes_of(uy, uz, half, z, low):
    depth = jnp.abs(uz - z)
    hz = hat(jnp.minimum(depth, 64.0 - depth))
    top = jnp.where(low, hat(uy - 4.0) * hz, 0.0)
    return [hat(uy - half) * hz, hat(uy - 2.0 - half) * hz, top]


def planes_across(pos):
    filled = jnp.concatenate([pos, jnp.zeros((5, ATOMS), F32)], axis=0)
    columns = filled.T
    wide = lambda d, scale: jnp.broadcast_to(columns[:, d : d + 1] * scale, (ATOMS, LANES))
    lane = lane_iota((1, LANES))
    half, z = (lane // 64).astype(F32), (lane % 64).astype(F32)
    return jnp.concatenate(planes_of(wide(1, 4.0), wide(2, float(MESH)), half, z, lane < 64), axis=1)


def planes_down(pos):
    row = lax.broadcasted_iota(jnp.int32, (LANES, 1), 0)
    half, z = (row // 64).astype(F32), (row % 64).astype(F32)
    uy, uz = pos[1:2, :] * 4.0, pos[2:3, :] * float(MESH)
    return jnp.concatenate(planes_of(uy, uz, half, z, row < 64), axis=0)


def spread_body(pos_ref, feat_ref, proj_ref, value_ref, pack_ref, out_ref):
    pos = rows_of(pos_ref)
    wh, wl = split(planes_across(pos))
    ux = pos[0:1, :] * 8.0
    charges = dot3(feat_ref[...], proj_ref[...]).T
    pack_body(feat_ref, pos_ref, value_ref, pack_ref)
    highs, lows = [], []
    for x in range(9):
        high, low = split(charges * hat(ux - float(x)))
        highs.append(high)
        lows.append(low)
    high = jnp.concatenate(highs, axis=0)
    low = jnp.concatenate(lows, axis=0)
    both = jnp.concatenate([wh[:, 256:320], wl[:, 256:320]], axis=1)
    wide = dot(high, jnp.concatenate([wh[:, :256], wl[:, :256], both], axis=1))
    last = wide[:, 512:]
    result = jnp.concatenate([wide[:, :256] + wide[:, 256:512], last + half_turn(last)], axis=1) + dot(low, wh)
    piece = lambda x, k: result[x * LANES : (x + 1) * LANES, k * LANES : (k + 1) * LANES]
    edge = [half_turn(piece(8, 0)), piece(8, 0), half_turn(piece(8, 1)), piece(8, 1), half_turn(piece(8, 2))]
    below = lane_iota((1, LANES)) < 64
    for x in range(8):
        out_ref[pl.ds(x, LANES, stride=ROWS), :] = piece(x, 0)
        out_ref[pl.ds(8 + x, LANES, stride=ROWS), :] = piece(x, 1)
        top = piece(x, 2)
        out_ref[pl.ds(16 + x, LANES, stride=ROWS), :] = jnp.where(below, top, edge[x]) if x < 5 else top


def real_basis():
    n = np.arange(MESH)
    rows = []
    for k in range(MESH):
        if k == 0:
            rows.append(np.full(MESH, 1.0 / 8.0))
        elif k == MESH // 2:
            rows.append(np.where(n % 2 == 0, 1.0, -1.0) / 8.0)
        elif k < MESH // 2:
            rows.append(np.cos(2 * np.pi * (k * n % MESH) / MESH) * math.sqrt(2.0) / 8.0)
        else:
            rows.append(np.sin(2 * np.pi * ((MESH - k) * n % MESH) / MESH) * math.sqrt(2.0) / 8.0)
    return np.stack(rows)


def halves(table):
    high = table.astype(np.float32).astype(ml_dtypes.bfloat16)
    low = (table - high.astype(np.float64)).astype(np.float32).astype(ml_dtypes.bfloat16)
    return high, low


def stacked(table):
    high, low = halves(table)
    return np.concatenate([high, low, high], axis=1)


def squared(table):
    high, low = halves(table)
    top = np.concatenate([high, low], axis=1)
    bottom = np.concatenate([high, np.zeros_like(low)], axis=1)
    return np.concatenate([top, bottom], axis=0)


def filter_tables():
    q = real_basis()
    y_forward = np.concatenate([q[:, 0::2], q[:, 1::2]], axis=0)
    y_back = np.concatenate([q.T[0::2], q.T[1::2]], axis=0)
    twice = np.kron(np.eye(2), q.T)
    tables = [stacked(q), stacked(y_forward), squared(twice), squared(twice.T), stacked(y_back), stacked(q.T)]
    wide = 2 * LANES
    filled = [np.pad(t.astype(np.float32), ((0, 0), (0, wide - t.shape[1]))) for t in tables]
    return np.concatenate(filled, axis=0).astype(ml_dtypes.bfloat16)


def stack_rows(x):
    high, low = split(x)
    return jnp.concatenate([high, high, low], axis=0)


def sum_halves(x):
    return x[:, :LANES] + x[:, LANES:]


def filter_body(
    screen_ref, smear_ref, in_ref, first_ref, table_ref, out_ref, turn_ref, edge_ref
):
    devices = 128
    low = lane_iota((1, LANES)) < 64
    place = lax.broadcasted_iota(jnp.int32, (devices, 1), 0) % 16

    side = [in_ref[pl.ds(16 + y, devices, stride=ROWS), :] for y in range(5)]
    corner = jnp.where(place == 0, pltpu.roll(side[4], 113, 0), pltpu.roll(side[4], 1, 0))
    side[0] = side[0] + corner
    for h in range(2):
        both = jnp.where(low, half_turn(side[2 * h]), side[2 * h + 1])
        edge_ref[h * devices : (h + 1) * devices, :] = pltpu.roll(both, 16, 0)

    first_row = lax.broadcasted_iota(jnp.int32, (8, 1), 0) == 0
    stacks = []
    for s in range(0, 16, 2):
        parts = []
        for k in range(4):
            d, h = s + k // 2, k % 2
            tiles = []
            for w in range(8):
                at = w * 16 + d
                tile = in_ref[at * ROWS + h * 8 : at * ROWS + h * 8 + 8, :]
                edge = edge_ref[h * devices + at : h * devices + at + 1, :]
                tile = tile + jnp.where(first_row, edge, 0.0)
                if h == 0:
                    below = (w * 16 + (d + 15) % 16) * ROWS + 16
                    tile = tile + jnp.where(low, in_ref[below : below + 8, :], 0.0)
                tiles.append(tile)
            parts.append(jnp.concatenate(tiles, axis=0))
        stacks.append(stack_rows(jnp.concatenate(parts, axis=1)))
    x_forward = first_ref[:, 0:192]
    for s, stack in zip(range(0, 16, 2), stacks):
        result = dot(x_forward, stack)
        for k in range(4):
            turn_ref[pl.ds(2 * s + k, MESH, stride=TURN), :] = result[:, k * LANES : (k + 1) * LANES]

    kappa = screen_ref[0]
    kappa_sq = kappa * kappa
    decay = -0.5 * smear_ref[0] * smear_ref[0]
    lane = lane_iota((1, LANES))
    fold = lambda k: jnp.minimum(k, MESH - k).astype(F32)
    nz = fold(lane % 64)
    ny = fold(lax.broadcasted_iota(jnp.int32, (MESH, 1), 0))
    scale = 4.0 * math.pi**2
    yz = (ny * ny + nz * nz) * scale
    y_forward, z_forward = table_ref[64:192, 0:96], table_ref[192:448, :]
    z_back, y_back = table_ref[448:704, :], table_ref[704:768, 0:192]
    group = 32
    for start in range(0, 32, group):
        planes = []
        for p in range(start, start + group, 2):
            pairs = jnp.concatenate(
                [turn_ref[(2 * p + k) * TURN : (2 * p + k) * TURN + 32, :] for k in range(4)], axis=1
            )
            result = dot(y_forward, stack_rows(pairs))
            for k in range(2):
                a = result[:, 2 * k * LANES : (2 * k + 1) * LANES]
                b = result[:, (2 * k + 1) * LANES : (2 * k + 2) * LANES]
                straight = jnp.where(low, a[:MESH], b[MESH:])
                planes.append(straight + half_turn(jnp.where(low, b[:MESH], a[MESH:])))
        stack = jnp.concatenate(planes, axis=0)
        stack = sum_halves(dot(jnp.concatenate(split(stack), axis=1), z_forward))
        gains = []
        for p in range(start, start + group):
            nx = fold(2 * p + lane // 64)
            square = yz + nx * nx * scale
            gains.append(kappa_sq * jnp.exp(square * decay) / (square + kappa_sq))
        stack = stack * jnp.concatenate(gains, axis=0)
        stack = sum_halves(dot(jnp.concatenate(split(stack), axis=1), z_back))
        for g in range(0, group, 4):
            pair = jnp.concatenate([stack[(g + k) * MESH : (g + k + 1) * MESH] for k in range(4)], axis=1)
            result = dot(y_back, stack_rows(pair))
            for k in range(4):
                p = start + g + k
                a = result[:32, k * LANES : (k + 1) * LANES]
                b = result[32:, k * LANES : (k + 1) * LANES]
                turn_ref[2 * p * TURN : 2 * p * TURN + 32, :] = jnp.where(low, a, half_turn(b))
                turn_ref[(2 * p + 1) * TURN : (2 * p + 1) * TURN + 32, :] = jnp.where(low, half_turn(a), b)

    x_back = table_ref[768:832, 0:192]
    for s in range(0, 16, 2):
        pair = jnp.concatenate(
            [turn_ref[pl.ds(2 * s + k, MESH, stride=TURN), :] for k in range(4)], axis=1
        )
        result = dot(x_back, stack_rows(pair))
        for w in range(8):
            for k in range(4):
                d, h = s + k // 2, k % 2
                at = (w * 16 + d) * ROWS
                tile = result[w * 8 : (w + 1) * 8, k * LANES : (k + 1) * LANES]
                out_ref[at + h * 8 : at + h * 8 + 8, :] = tile
                if h == 0:
                    below = (w * 16 + (d + 15) % 16) * ROWS + 16
                    out_ref[below : below + 8, :] = jnp.where(low, tile, 0.0)

    ahead = [pltpu.roll(out_ref[pl.ds(8 * h, devices, stride=ROWS), :], 112, 0) for h in range(2)]
    turned = [half_turn(x) for x in ahead]
    corner = jnp.where(place == 15, pltpu.roll(turned[0], 15, 0), pltpu.roll(turned[0], 127, 0))
    for y, high in enumerate([turned[0], ahead[0], turned[1], ahead[1], corner]):
        rows = pl.ds(16 + y, devices, stride=ROWS)
        out_ref[rows, :] = jnp.where(low, out_ref[rows, :], high)


ENVELOPE = (
    0.9999999991137324,
    -0.4674010362718563,
    0.0945531128786198,
    -0.011119339660821159,
    0.0008600612678157039,
    -4.252312938118321e-05,
)


def short_body(
    blocks, units, packs, extra, live_ref, pos_ref, part_ref, mix_ref, *rest
):
    packs, rest = rest[:packs], rest[packs:]
    *rest, val_ref, win_ref, own_ref = rest
    given = len(extra.operands)
    out_ref = rest[given]
    extra.body(*rest[:given], *rest[given + 1 :])
    lane = lane_iota((1, LANES))
    filled = jnp.concatenate([rows_of(pos_ref), jnp.zeros((5, ATOMS), F32)], axis=0)
    columns = filled.T
    for d, scale in ((0, 0.125), (1, 0.0625), (2, 1.0)):
        own_ref[d * ATOMS : (d + 1) * ATOMS, :] = jnp.broadcast_to(
            columns[:, d : d + 1] * scale, (ATOMS, LANES)
        )

    row = lax.broadcasted_iota(jnp.int32, (16, 1), 0)
    axis, tile = row // 4, row % 4
    pick = lambda x, y, z: jnp.where(axis == 0, x, jnp.where(axis == 1, y, z))
    scale = pick(0.125, 0.0625, 1.0)
    wrap_low = jnp.where((axis == 2) & (tile == 0), -1.0, 0.0)
    wrap_high = jnp.where((axis == 2) & (tile == 3), 1.0, 0.0)
    for k, nb in enumerate(blocks):
        dx, dy = nb // 3 - 1, nb % 3 - 1
        ref, base = packs[0 if dx < 1 else -1], (dy + 1) * PACK
        high, low = split(ref[base : base + ATOMS, :])
        both = jnp.concatenate([high, low], axis=1)
        val_ref[k, 32 : 32 + ATOMS, :] = both
        val_ref[k, 0:32, :] = both[ATOMS - 32 :, :]
        val_ref[k, ATOMS + 32 :, :] = both[:32, :]
        pos = (ref[base + ATOMS : base + PACK, :] + pick(float(dx), float(dy), 0.0)) * scale
        up = pltpu.roll(pos, 32, 1)
        before = jnp.where(tile == 0, pltpu.roll(up, 13, 0), pltpu.roll(up, 1, 0)) + wrap_low
        win_ref[k, 0] = jnp.where(lane < 32, before, up)
        down = pltpu.roll(pos, 96, 1)
        after = jnp.where(tile == 3, pltpu.roll(down, 3, 0), pltpu.roll(down, 15, 0)) + wrap_high
        win_ref[k, 1] = jnp.where(lane < 96, down, after)

    me = lax.broadcasted_iota(jnp.int32, (CHUNK, LANES), 0) + 32
    itself = (me == lane_iota((CHUNK, LANES))).astype(F32)
    zero = jnp.zeros((LANES, LANES), BF)
    half = BASES // 2

    def chunk(acc_a, acc_b, m, carry):
        t = m // 2
        parity = m % 2
        even = parity == 0
        tile_a = jnp.where(even, (t + 3) % 4, t)
        tile_b = jnp.where(even, t, (t + 1) % 4)
        from_first = lane < jnp.where(even, 32, 96)
        start = pl.multiple_of(m * CHUNK, CHUNK)

        for k, nb in enumerate(blocks):
            live_a = live_ref[t, nb * 4 + tile_a]
            live_b = live_ref[t, nb * 4 + tile_b]

            @pl.when(live_a + live_b > 0)
            def _(k=k, nb=nb, live_a=live_a, live_b=live_b):
                values = val_ref[k, pl.ds(start, LANES), :]
                rhs = jnp.concatenate(
                    [values, jnp.concatenate([values[:, :LANES], zero], axis=1)], axis=0
                )
                for unit in range(2):
                    pltpu.matmul_push_rhs(rhs, 0, unit)
                far_a = (1 - live_a).astype(F32) * FAR
                far_b = (1 - live_b).astype(F32) * FAR
                take = lambda d: win_ref[k, parity, pl.ds(4 * d + t, 1), :]
                xj = take(0) + jnp.where(from_first, far_a, far_b)
                dx = xj - own_ref[pl.ds(start, CHUNK), :]
                dy = take(1) - own_ref[pl.ds(ATOMS + start, CHUNK), :]
                dz = take(2) - own_ref[pl.ds(2 * ATOMS + start, CHUNK), :]
                s = (dx * dx + dy * dy + dz * dz) * (1.0 / CUTOFF**2)
                if nb == 4:
                    s = jnp.maximum(s, itself)
                s = jnp.minimum(s, 1.0)
                q = s * lax.rsqrt(jnp.maximum(s, 1e-30))
                v = q * float(BASES - 1) - float(MID)
                env = jnp.full_like(s, ENVELOPE[-1])
                for c in ENVELOPE[-2::-1]:
                    env = env * s + c
                rest = 1.0 - s
                middle = jnp.exp(-0.5 * v * v) * (env * (rest * rest))
                up, down = jnp.exp(v), jnp.exp(-v)
                terms = [None] * BASES
                terms[MID] = middle
                for b in range(MID + 1, BASES):
                    terms[b] = terms[b - 1] * up
                for b in range(MID - 1, -1, -1):
                    terms[b] = terms[b + 1] * down
                sides = [jnp.concatenate(split(x), axis=1) for x in terms]
                pltpu.matmul_acc_lhs(acc_a, jnp.concatenate(sides[:half], axis=0), load_staged_rhs=0)
                pltpu.matmul_acc_lhs(acc_b, jnp.concatenate(sides[half:], axis=0), load_staged_rhs=0)

        total = part_ref[pl.ds(start, CHUNK), :]
        for unit, acc in enumerate((acc_a, acc_b)):
            found = sum_halves(pltpu.matmul_pop(acc))
            for j in range(half):
                b = unit * half + j
                weight = mix_ref[b : b + 1, :] * math.exp(-0.5 * (b - MID) ** 2)
                total = total + found[j * CHUNK : (j + 1) * CHUNK, :] * weight
        out_ref[pl.ds(start, CHUNK), :] = total
        return carry

    pl.run_scoped(
        lambda acc_a, acc_b: lax.fori_loop(0, CHUNKS, functools.partial(chunk, acc_a, acc_b), 0), *units
    )


def silu(v):
    half = 0.5 * v
    return half + half * jnp.tanh(half)


def stack_lanes(x):
    high, low = split(x)
    return jnp.concatenate([high, low, high], axis=1)


def beside(x):
    return jnp.concatenate(split(x), axis=1)


def mesh_weights_body(gain_ref, up_ref, down_ref, out_ref):
    out_ref[:, 0:256] = beside(up_ref[...].T * gain_ref[...])
    high, low = split(down_ref[...].T)
    out_ref[0:128, 256:512] = high
    out_ref[128:256, 256:512] = low


def prepare_body(pos_ref, long_ref, again_ref, aup_ref, adown_ref, out_ref, hat_out):
    out_ref[1024:1152, :] = beside((aup_ref[...].T * again_ref[...]).T)
    out_ref[1152:1408, 0:256] = beside(adown_ref[...])
    out_ref[1152:1280, 256:512] = beside(long_ref[...])
    pos = rows_of(pos_ref)
    high, low = split(planes_down(pos))
    main = 2 * LANES
    pieces = [high[:main], high[:main], low[:main], high[main : main + 64], high[main : main + 64], low[main:]]
    out_ref[0:1024, :] = jnp.concatenate(pieces, axis=0)
    ux = pos[0:1, :] * 8.0
    hats = [hat(ux - float(x)) for x in range(9)] + [jnp.zeros((7, ATOMS), F32)]
    hat_out[...] = jnp.concatenate(hats, axis=0)


def dot_beside(x, pair):
    high, low = split(x)
    width = pair.shape[1] // 2
    wide = dot(high, pair)
    return wide[:, :width] + (wide[:, width:] + dot(low, pair[:, :width]))


def final_body(msg_ref, in_ref, mesh_ref, set_ref, hat_ref, out_ref):
    mesh_out, stacks = [], []
    width = 12
    for r in range(0, ROWS, width):
        cells = jnp.concatenate(
            [in_ref[pl.ds(r + k, LANES, stride=ROWS), :] for k in range(width)], axis=1
        )
        inverse = lax.rsqrt(jnp.mean(cells * cells, axis=0, keepdims=True) + 1e-06)
        stacks.append(stack_rows(cells * inverse))
    first = mesh_ref[...]
    up = jnp.concatenate([first[:, :256], first[:, :128]], axis=1)
    down = jnp.concatenate([first[:128, 256:], first[128:, 256:], first[:128, 256:]], axis=1)
    for stack in stacks:
        result = dot(down, stack_rows(silu(dot(up, stack))))
        mesh_out += [result[:, k * LANES : (k + 1) * LANES] for k in range(width)]
    below = lane_iota((1, LANES)) < 64
    top = mesh_out[16:]
    mixed = lambda a, b: jnp.where(below, half_turn(a), b)
    edge = [mixed(top[0], top[1]), mixed(top[2], top[3]), half_turn(top[4])]
    stacks = []
    for x in range(9):
        first, second, last = edge if x == 8 else [mesh_out[x], mesh_out[8 + x], top[x]]
        high, low = split(jnp.concatenate([first, second], axis=1))
        rounded = last.astype(BF).astype(F32)
        both = jnp.where(below, rounded, half_turn(last - rounded))
        stacks.append(jnp.concatenate([high, low, high, both.astype(BF), rounded.astype(BF)], axis=1))
    found = dot(jnp.concatenate(stacks, axis=0), set_ref[0:1024, :])
    total = None
    for x in range(9):
        term = found[x * LANES : (x + 1) * LANES] * hat_ref[x : x + 1, :]
        total = term if total is None else total + term
    summed = msg_ref[...] + dot_beside(total.T, set_ref[1152:1280, 256:512])
    inverse = lax.rsqrt(jnp.mean(summed * summed, axis=1, keepdims=True) + 1e-06)
    hidden = silu(dot_beside(summed * inverse, set_ref[1024:1152, :]))
    out_ref[...] = summed + dot_beside(hidden, set_ref[1152:1408, 0:256])


def whole():
    return pl.BlockSpec(memory_space=pltpu.VMEM)


def scalars():
    return pl.BlockSpec(memory_space=pltpu.SMEM)


def in_hbm(x):
    return pltpu.with_memory_space_constraint(x, pltpu.HBM)


def remote():
    return pl.BlockSpec(memory_space=pltpu.HBM)


class Fetched:
    def __init__(self, source, target, semaphore, first, cuts):
        self.target = target
        self.copies = []
        for k, (low, high) in enumerate(zip(cuts[:-1], cuts[1:])):
            rows = pl.ds(low, high - low)
            copy = pltpu.make_async_copy(source.at[rows], target.at[rows], semaphore.at[first + k])
            copy.start()
            self.copies.append([low, high, copy])

    def __getitem__(self, index):
        rows = index[0] if isinstance(index, tuple) else index
        if isinstance(rows, slice):
            start, stop = rows.start or 0, self.target.shape[0] if rows.stop is None else rows.stop
        elif isinstance(rows, int):
            start, stop = rows, rows + 1
        else:
            start, stop = 0, self.target.shape[0]
        for entry in self.copies:
            if entry[2] is not None and entry[0] < stop and entry[1] > start:
                entry[2].wait()
                entry[2] = None
        return self.target[index]


def call(body, name, shapes, places, scratch, cost, operands, cuts={}):
    specs = {"v": whole, "s": scalars, "h": remote}
    far = [i for i, p in enumerate(places) if p == "h"]
    buffers = [pltpu.VMEM(operands[i].shape, operands[i].dtype) for i in far]
    count = len(places)
    parts = [cuts.get(i, (0, operands[i].shape[0])) for i in far]
    firsts = [sum(len(p) - 1 for p in parts[:k]) for k in range(len(far) + 1)]

    def kernel(*refs):
        inputs, rest = list(refs[:count]), refs[count:]
        if far:
            held, semaphores = rest[-len(far) - 1 : -1], rest[-1]
            for k, i in enumerate(far):
                inputs[i] = Fetched(inputs[i], held[k], semaphores, firsts[k], parts[k])
            rest = rest[: -len(far) - 1]
        body(*inputs, *rest)

    extra = buffers + [pltpu.SemaphoreType.DMA((firsts[-1],))] if far else []
    return pl.pallas_call(
        kernel,
        out_shape=[jax.ShapeDtypeStruct(x, F32) if isinstance(x, tuple) else x for x in shapes],
        in_specs=[specs[p]() for p in places],
        out_specs=[whole()] * len(shapes),
        scratch_shapes=list(scratch) + extra,
        name=name,
        compiler_params=pltpu.CompilerParams(vmem_limit_bytes=LIMIT),
        cost_estimate=pl.CostEstimate(flops=cost, bytes_accessed=4 * 1024 * 1024, transcendentals=0),
    )(*operands)


def spread_call(*operands):
    operands = [in_hbm(x) for x in operands]
    shapes = [(PACK, LANES), (LANES * ROWS, LANES)]
    return call(spread_body, "spread", shapes, "hhhh", [], 1_200_000_000, operands)


def prepare_call(*operands):
    shapes = [jax.ShapeDtypeStruct((1408, 512), BF), (16, ATOMS)]
    return call(prepare_body, "prepare", shapes, "v" * 5, [], PREPARE_COST, operands)


def first_table_extra():
    table = jnp.asarray(filter_tables()[:MESH])
    return Extra(copy_body, [jax.ShapeDtypeStruct(table.shape, BF)], (table,))


def copy_body(source_ref, target_ref):
    target_ref[...] = source_ref[...]


def filter_call(screening, smearing, received, first):
    scratch = [pltpu.VMEM((MESH * TURN, LANES), F32), pltpu.VMEM((256, LANES), F32)]
    operands = (screening, smearing, received, first, in_hbm(jnp.asarray(filter_tables())))
    shapes = [(LANES * ROWS, LANES)]
    return call(filter_body, "filter", shapes, "ssvvh", scratch, 2_000_000_000, operands)[0]


class Extra:
    def __init__(self, body, shapes, operands):
        self.body, self.shapes, self.operands = body, shapes, operands


def short_call(mesh, blocks, extra, live, pos, part, mix, *packs):
    with jax.sharding.use_abstract_mesh(mesh.abstract_mesh):
        units = [pltpu.ACC(i)((BASES // 2 * CHUNK, 2 * LANES), F32) for i in range(2)]
    scratch = [
        pltpu.VMEM((len(blocks), ATOMS + 64, 2 * LANES), BF),
        pltpu.VMEM((len(blocks), 2, 16, LANES), F32),
        pltpu.VMEM((3 * ATOMS, LANES), F32),
    ]
    body = functools.partial(short_body, blocks, units, len(packs), extra)
    operands = (live, pos, part, mix, *packs, *extra.operands)
    places = "s" + "v" * (len(operands) - 1)
    shapes = [(ATOMS, LANES)] + extra.shapes
    return call(body, "short_range", shapes, places, scratch, SHORT_COST, operands)


def final_call(messages, returned, mesh, weights, hats):
    operands = (messages, returned, mesh, in_hbm(weights), in_hbm(hats))
    cuts = {3: (0, 1024, 1408)}
    return call(final_body, "final", [(ATOMS, LANES)], "vvvhh", [], 2_400_000_000, operands, cuts)[0]


def passed_along(array, axis, by):
    count = lax.axis_size(axis)
    return lax.ppermute(array, axis, [(i, (i + by) % count) for i in range(count)])


def on_device(
    mesh,
    features,
    positions,
    tile_lists,
    value_proj,
    radial_mix,
    charge_proj,
    screening,
    smearing,
    mesh_gain,
    mesh_up,
    mesh_down,
    long_proj,
    atom_gain,
    atom_up,
    atom_down,
):
    feat, pos = features[0, 0], positions.reshape(3, 1, ATOMS)
    everyone = ("wide", "sixteen")
    packed, spread = spread_call(pos, feat, charge_proj, value_proj)
    below = passed_along(packed, "sixteen", 1)
    above = passed_along(packed, "sixteen", -1)
    received = lax.all_to_all(spread, everyone, split_axis=0, concat_axis=0, tiled=True)
    near = jnp.concatenate([below, packed, above], axis=0)
    left = passed_along(near, "wide", 1)
    right = passed_along(near, "wide", -1)
    codes = jnp.arange(36, dtype=jnp.int32)
    live = jnp.any(tile_lists[0, 0][:, :, None] == codes, axis=1).astype(jnp.int32)
    prepared = prepare_call(pos, long_proj, atom_gain[None], atom_up, atom_down)
    part, table = short_call(mesh, (3, 4, 5), first_table_extra(), live, pos, feat, radial_mix, near)
    received, part, table = lax.optimization_barrier((received, part, table))
    filtered = filter_call(screening, smearing, received, table)
    returned = lax.all_to_all(filtered, everyone, split_axis=0, concat_axis=0, tiled=True)
    shape = jax.ShapeDtypeStruct((256, 512), BF)
    weights = Extra(mesh_weights_body, [shape], (mesh_gain[None], mesh_up, mesh_down))
    messages, mesh_weights = short_call(
        mesh, (0, 1, 2, 6, 7, 8), weights, live, pos, part, radial_mix, left, right
    )
    updated = final_call(messages, returned, mesh_weights, *prepared)
    return updated[None, None]


def solution(mesh):
    block = P("wide", "sixteen", None, None)
    channel = P(("wide", "sixteen"))
    in_specs = (block,) * 3 + (P(),) * 3 + (channel,) * 2 + (P(),) * 7
    return jax.shard_map(
        functools.partial(on_device, mesh), mesh=mesh, in_specs=in_specs, out_specs=block, check_vma=False
    )
```

```python
import functools
import math

import jax
import jax.numpy as jnp
import ml_dtypes
import numpy as np
from jax import lax
from jax.experimental import pallas as pl
from jax.experimental.pallas import tpu as pltpu
from jax.sharding import PartitionSpec as P

F32 = jnp.float32
BF = jnp.bfloat16
MESH = 64
LANES = 128
ATOMS = 512
CHUNK = 64
CHUNKS = ATOMS // CHUNK
BASES = 16
ROWS = 24
PACK = 528
TURN = 40
FAR = 1000.0
CUTOFF = 0.05
MID = 8
LIMIT = 32 * 1024 * 1024
SHORT_COST = 24_000_000_000
PACK_COST = 50_000_000
PREPARE_COST = 1_000


def split(x):
    hi = x.astype(BF)
    return hi, (x - hi.astype(F32)).astype(BF)


def dot(a, b):
    return jnp.dot(a, b, preferred_element_type=F32)


def dot_nt(a, b):
    return lax.dot_general(a, b, (((1,), (1,)), ((), ())), preferred_element_type=F32)


def dot3(a, b):
    ah, al = split(a)
    bh, bl = split(b)
    return dot(ah, bh) + (dot(ah, bl) + dot(al, bh))


def rows_of(pos_ref):
    return jnp.concatenate([pos_ref[0], pos_ref[1], pos_ref[2]], axis=0)


def lane_iota(shape):
    return lax.broadcasted_iota(jnp.int32, shape, len(shape) - 1)


def half_turn(x):
    return pltpu.roll(x, 64, x.ndim - 1)


def pack_body(feat_ref, pos_ref, proj_ref, out_ref):
    for d in range(3):
        pos = pos_ref[d]
        for t in range(4):
            row = ATOMS + 4 * d + t
            out_ref[row : row + 1, :] = pos[:, t * LANES : (t + 1) * LANES]
    out_ref[ATOMS + 12 : PACK, :] = jnp.zeros((PACK - ATOMS - 12, LANES), F32)
    out_ref[0:ATOMS, :] = dot3(feat_ref[...], proj_ref[...])


def hat(distance):
    return jnp.maximum(1.0 - jnp.abs(distance), 0.0)


def planes_of(uy, uz, half, z, low):
    depth = jnp.abs(uz - z)
    hz = hat(jnp.minimum(depth, 64.0 - depth))
    top = jnp.where(low, hat(uy - 4.0) * hz, 0.0)
    return [hat(uy - half) * hz, hat(uy - 2.0 - half) * hz, top]


def planes_across(pos):
    filled = jnp.concatenate([pos, jnp.zeros((5, ATOMS), F32)], axis=0)
    columns = filled.T
    wide = lambda d, scale: jnp.broadcast_to(columns[:, d : d + 1] * scale, (ATOMS, LANES))
    lane = lane_iota((1, LANES))
    half, z = (lane // 64).astype(F32), (lane % 64).astype(F32)
    return jnp.concatenate(planes_of(wide(1, 4.0), wide(2, float(MESH)), half, z, lane < 64), axis=1)


def planes_down(pos):
    row = lax.broadcasted_iota(jnp.int32, (LANES, 1), 0)
    half, z = (row // 64).astype(F32), (row % 64).astype(F32)
    uy, uz = pos[1:2, :] * 4.0, pos[2:3, :] * float(MESH)
    return jnp.concatenate(planes_of(uy, uz, half, z, row < 64), axis=0)


def spread_body(pos_ref, feat_ref, proj_ref, value_ref, pack_ref, out_ref):
    pos = rows_of(pos_ref)
    wh, wl = split(planes_across(pos))
    ux = pos[0:1, :] * 8.0
    charges = dot3(feat_ref[...], proj_ref[...]).T
    pack_body(feat_ref, pos_ref, value_ref, pack_ref)
    highs, lows = [], []
    for x in range(9):
        high, low = split(charges * hat(ux - float(x)))
        highs.append(high)
        lows.append(low)
    high = jnp.concatenate(highs, axis=0)
    low = jnp.concatenate(lows, axis=0)
    both = jnp.concatenate([wh[:, 256:320], wl[:, 256:320]], axis=1)
    wide = dot(high, jnp.concatenate([wh[:, :256], wl[:, :256], both], axis=1))
    last = wide[:, 512:]
    result = jnp.concatenate([wide[:, :256] + wide[:, 256:512], last + half_turn(last)], axis=1) + dot(low, wh)
    piece = lambda x, k: result[x * LANES : (x + 1) * LANES, k * LANES : (k + 1) * LANES]
    edge = [half_turn(piece(8, 0)), piece(8, 0), half_turn(piece(8, 1)), piece(8, 1), half_turn(piece(8, 2))]
    below = lane_iota((1, LANES)) < 64
    for x in range(8):
        out_ref[pl.ds(x, LANES, stride=ROWS), :] = piece(x, 0)
        out_ref[pl.ds(8 + x, LANES, stride=ROWS), :] = piece(x, 1)
        top = piece(x, 2)
        out_ref[pl.ds(16 + x, LANES, stride=ROWS), :] = jnp.where(below, top, edge[x]) if x < 5 else top


def real_basis():
    n = np.arange(MESH)
    rows = []
    for k in range(MESH):
        if k == 0:
            rows.append(np.full(MESH, 1.0 / 8.0))
        elif k == MESH // 2:
            rows.append(np.where(n % 2 == 0, 1.0, -1.0) / 8.0)
        elif k < MESH // 2:
            rows.append(np.cos(2 * np.pi * (k * n % MESH) / MESH) * math.sqrt(2.0) / 8.0)
        else:
            rows.append(np.sin(2 * np.pi * ((MESH - k) * n % MESH) / MESH) * math.sqrt(2.0) / 8.0)
    return np.stack(rows)


def halves(table):
    high = table.astype(np.float32).astype(ml_dtypes.bfloat16)
    low = (table - high.astype(np.float64)).astype(np.float32).astype(ml_dtypes.bfloat16)
    return high, low


def stacked(table):
    high, low = halves(table)
    return np.concatenate([high, low, high], axis=1)


def squared(table):
    high, low = halves(table)
    top = np.concatenate([high, low], axis=1)
    bottom = np.concatenate([high, np.zeros_like(low)], axis=1)
    return np.concatenate([top, bottom], axis=0)


def filter_tables():
    q = real_basis()
    y_forward = np.concatenate([q[:, 0::2], q[:, 1::2]], axis=0)
    y_back = np.concatenate([q.T[0::2], q.T[1::2]], axis=0)
    twice = np.kron(np.eye(2), q.T)
    tables = [stacked(q), stacked(y_forward), squared(twice), squared(twice.T), stacked(y_back), stacked(q.T)]
    wide = 2 * LANES
    filled = [np.pad(t.astype(np.float32), ((0, 0), (0, wide - t.shape[1]))) for t in tables]
    return np.concatenate(filled, axis=0).astype(ml_dtypes.bfloat16)


def stack_rows(x):
    high, low = split(x)
    return jnp.concatenate([high, high, low], axis=0)


def sum_halves(x):
    return x[:, :LANES] + x[:, LANES:]


def filter_body(
    screen_ref, smear_ref, in_ref, first_ref, table_ref, out_ref, turn_ref, edge_ref
):
    devices = 128
    low = lane_iota((1, LANES)) < 64
    place = lax.broadcasted_iota(jnp.int32, (devices, 1), 0) % 16

    side = [in_ref[pl.ds(16 + y, devices, stride=ROWS), :] for y in range(5)]
    corner = jnp.where(place == 0, pltpu.roll(side[4], 113, 0), pltpu.roll(side[4], 1, 0))
    side[0] = side[0] + corner
    for h in range(2):
        both = jnp.where(low, half_turn(side[2 * h]), side[2 * h + 1])
        edge_ref[h * devices : (h + 1) * devices, :] = pltpu.roll(both, 16, 0)

    first_row = lax.broadcasted_iota(jnp.int32, (8, 1), 0) == 0
    stacks = []
    for s in range(0, 16, 2):
        parts = []
        for k in range(4):
            d, h = s + k // 2, k % 2
            tiles = []
            for w in range(8):
                at = w * 16 + d
                tile = in_ref[at * ROWS + h * 8 : at * ROWS + h * 8 + 8, :]
                edge = edge_ref[h * devices + at : h * devices + at + 1, :]
                tile = tile + jnp.where(first_row, edge, 0.0)
                if h == 0:
                    below = (w * 16 + (d + 15) % 16) * ROWS + 16
                    tile = tile + jnp.where(low, in_ref[below : below + 8, :], 0.0)
                tiles.append(tile)
            parts.append(jnp.concatenate(tiles, axis=0))
        stacks.append(stack_rows(jnp.concatenate(parts, axis=1)))
    x_forward = first_ref[:, 0:192]
    for s, stack in zip(range(0, 16, 2), stacks):
        result = dot(x_forward, stack)
        for k in range(4):
            turn_ref[pl.ds(2 * s + k, MESH, stride=TURN), :] = result[:, k * LANES : (k + 1) * LANES]

    kappa = screen_ref[0]
    kappa_sq = kappa * kappa
    decay = -0.5 * smear_ref[0] * smear_ref[0]
    lane = lane_iota((1, LANES))
    fold = lambda k: jnp.minimum(k, MESH - k).astype(F32)
    nz = fold(lane % 64)
    ny = fold(lax.broadcasted_iota(jnp.int32, (MESH, 1), 0))
    scale = 4.0 * math.pi**2
    yz = (ny * ny + nz * nz) * scale
    y_forward, z_forward = table_ref[64:192, 0:96], table_ref[192:448, :]
    z_back, y_back = table_ref[448:704, :], table_ref[704:768, 0:192]
    group = 32
    for start in range(0, 32, group):
        planes = []
        for p in range(start, start + group, 2):
            pairs = jnp.concatenate(
                [turn_ref[(2 * p + k) * TURN : (2 * p + k) * TURN + 32, :] for k in range(4)], axis=1
            )
            result = dot(y_forward, stack_rows(pairs))
            for k in range(2):
                a = result[:, 2 * k * LANES : (2 * k + 1) * LANES]
                b = result[:, (2 * k + 1) * LANES : (2 * k + 2) * LANES]
                straight = jnp.where(low, a[:MESH], b[MESH:])
                planes.append(straight + half_turn(jnp.where(low, b[:MESH], a[MESH:])))
        stack = jnp.concatenate(planes, axis=0)
        stack = sum_halves(dot(jnp.concatenate(split(stack), axis=1), z_forward))
        gains = []
        for p in range(start, start + group):
            nx = fold(2 * p + lane // 64)
            square = yz + nx * nx * scale
            gains.append(kappa_sq * jnp.exp(square * decay) / (square + kappa_sq))
        stack = stack * jnp.concatenate(gains, axis=0)
        stack = sum_halves(dot(jnp.concatenate(split(stack), axis=1), z_back))
        for g in range(0, group, 4):
            pair = jnp.concatenate([stack[(g + k) * MESH : (g + k + 1) * MESH] for k in range(4)], axis=1)
            result = dot(y_back, stack_rows(pair))
            for k in range(4):
                p = start + g + k
                a = result[:32, k * LANES : (k + 1) * LANES]
                b = result[32:, k * LANES : (k + 1) * LANES]
                turn_ref[2 * p * TURN : 2 * p * TURN + 32, :] = jnp.where(low, a, half_turn(b))
                turn_ref[(2 * p + 1) * TURN : (2 * p + 1) * TURN + 32, :] = jnp.where(low, half_turn(a), b)

    x_back = table_ref[768:832, 0:192]
    for s in range(0, 16, 2):
        pair = jnp.concatenate(
            [turn_ref[pl.ds(2 * s + k, MESH, stride=TURN), :] for k in range(4)], axis=1
        )
        result = dot(x_back, stack_rows(pair))
        for w in range(8):
            for k in range(4):
                d, h = s + k // 2, k % 2
                at = (w * 16 + d) * ROWS
                tile = result[w * 8 : (w + 1) * 8, k * LANES : (k + 1) * LANES]
                out_ref[at + h * 8 : at + h * 8 + 8, :] = tile
                if h == 0:
                    below = (w * 16 + (d + 15) % 16) * ROWS + 16
                    out_ref[below : below + 8, :] = jnp.where(low, tile, 0.0)

    ahead = [pltpu.roll(out_ref[pl.ds(8 * h, devices, stride=ROWS), :], 112, 0) for h in range(2)]
    turned = [half_turn(x) for x in ahead]
    corner = jnp.where(place == 15, pltpu.roll(turned[0], 15, 0), pltpu.roll(turned[0], 127, 0))
    for y, high in enumerate([turned[0], ahead[0], turned[1], ahead[1], corner]):
        rows = pl.ds(16 + y, devices, stride=ROWS)
        out_ref[rows, :] = jnp.where(low, out_ref[rows, :], high)


ENVELOPE = (
    0.9999999991137324,
    -0.4674010362718563,
    0.0945531128786198,
    -0.011119339660821159,
    0.0008600612678157039,
    -4.252312938118321e-05,
)


def short_body(
    blocks, units, packs, extra, live_ref, pos_ref, part_ref, mix_ref, *rest
):
    packs, rest = rest[:packs], rest[packs:]
    *rest, val_ref, win_ref, own_ref = rest
    given = len(extra.operands)
    out_ref = rest[given]
    extra.body(*rest[:given], *rest[given + 1 :])
    lane = lane_iota((1, LANES))
    filled = jnp.concatenate([rows_of(pos_ref), jnp.zeros((5, ATOMS), F32)], axis=0)
    columns = filled.T
    for d, scale in ((0, 0.125), (1, 0.0625), (2, 1.0)):
        own_ref[d * ATOMS : (d + 1) * ATOMS, :] = jnp.broadcast_to(
            columns[:, d : d + 1] * scale, (ATOMS, LANES)
        )

    row = lax.broadcasted_iota(jnp.int32, (16, 1), 0)
    axis, tile = row // 4, row % 4
    pick = lambda x, y, z: jnp.where(axis == 0, x, jnp.where(axis == 1, y, z))
    scale = pick(0.125, 0.0625, 1.0)
    wrap_low = jnp.where((axis == 2) & (tile == 0), -1.0, 0.0)
    wrap_high = jnp.where((axis == 2) & (tile == 3), 1.0, 0.0)
    for k, nb in enumerate(blocks):
        dx, dy = nb // 3 - 1, nb % 3 - 1
        ref, base = packs[0 if dx < 1 else -1], (dy + 1) * PACK
        high, low = split(ref[base : base + ATOMS, :])
        both = jnp.concatenate([high, low], axis=1)
        val_ref[k, 32 : 32 + ATOMS, :] = both
        val_ref[k, 0:32, :] = both[ATOMS - 32 :, :]
        val_ref[k, ATOMS + 32 :, :] = both[:32, :]
        pos = (ref[base + ATOMS : base + PACK, :] + pick(float(dx), float(dy), 0.0)) * scale
        up = pltpu.roll(pos, 32, 1)
        before = jnp.where(tile == 0, pltpu.roll(up, 13, 0), pltpu.roll(up, 1, 0)) + wrap_low
        win_ref[k, 0] = jnp.where(lane < 32, before, up)
        down = pltpu.roll(pos, 96, 1)
        after = jnp.where(tile == 3, pltpu.roll(down, 3, 0), pltpu.roll(down, 15, 0)) + wrap_high
        win_ref[k, 1] = jnp.where(lane < 96, down, after)

    me = lax.broadcasted_iota(jnp.int32, (CHUNK, LANES), 0) + 32
    itself = (me == lane_iota((CHUNK, LANES))).astype(F32)
    zero = jnp.zeros((LANES, LANES), BF)
    half = BASES // 2

    def chunk(acc_a, acc_b, m, carry):
        t = m // 2
        parity = m % 2
        even = parity == 0
        tile_a = jnp.where(even, (t + 3) % 4, t)
        tile_b = jnp.where(even, t, (t + 1) % 4)
        from_first = lane < jnp.where(even, 32, 96)
        start = pl.multiple_of(m * CHUNK, CHUNK)

        for k, nb in enumerate(blocks):
            live_a = live_ref[t, nb * 4 + tile_a]
            live_b = live_ref[t, nb * 4 + tile_b]

            @pl.when(live_a + live_b > 0)
            def _(k=k, nb=nb, live_a=live_a, live_b=live_b):
                values = val_ref[k, pl.ds(start, LANES), :]
                rhs = jnp.concatenate(
                    [values, jnp.concatenate([values[:, :LANES], zero], axis=1)], axis=0
                )
                for unit in range(2):
                    pltpu.matmul_push_rhs(rhs, 0, unit)
                far_a = (1 - live_a).astype(F32) * FAR
                far_b = (1 - live_b).astype(F32) * FAR
                take = lambda d: win_ref[k, parity, pl.ds(4 * d + t, 1), :]
                xj = take(0) + jnp.where(from_first, far_a, far_b)
                dx = xj - own_ref[pl.ds(start, CHUNK), :]
                dy = take(1) - own_ref[pl.ds(ATOMS + start, CHUNK), :]
                dz = take(2) - own_ref[pl.ds(2 * ATOMS + start, CHUNK), :]
                s = (dx * dx + dy * dy + dz * dz) * (1.0 / CUTOFF**2)
                if nb == 4:
                    s = jnp.maximum(s, itself)
                s = jnp.minimum(s, 1.0)
                q = s * lax.rsqrt(jnp.maximum(s, 1e-30))
                v = q * float(BASES - 1) - float(MID)
                env = jnp.full_like(s, ENVELOPE[-1])
                for c in ENVELOPE[-2::-1]:
                    env = env * s + c
                rest = 1.0 - s
                middle = jnp.exp(-0.5 * v * v) * (env * (rest * rest))
                up, down = jnp.exp(v), jnp.exp(-v)
                terms = [None] * BASES
                terms[MID] = middle
                for b in range(MID + 1, BASES):
                    terms[b] = terms[b - 1] * up
                for b in range(MID - 1, -1, -1):
                    terms[b] = terms[b + 1] * down
                sides = [jnp.concatenate(split(x), axis=1) for x in terms]
                pltpu.matmul_acc_lhs(acc_a, jnp.concatenate(sides[:half], axis=0), load_staged_rhs=0)
                pltpu.matmul_acc_lhs(acc_b, jnp.concatenate(sides[half:], axis=0), load_staged_rhs=0)

        total = part_ref[pl.ds(start, CHUNK), :]
        for unit, acc in enumerate((acc_a, acc_b)):
            found = sum_halves(pltpu.matmul_pop(acc))
            for j in range(half):
                b = unit * half + j
                weight = mix_ref[b : b + 1, :] * math.exp(-0.5 * (b - MID) ** 2)
                total = total + found[j * CHUNK : (j + 1) * CHUNK, :] * weight
        out_ref[pl.ds(start, CHUNK), :] = total
        return carry

    pl.run_scoped(
        lambda acc_a, acc_b: lax.fori_loop(0, CHUNKS, functools.partial(chunk, acc_a, acc_b), 0), *units
    )


def silu(v):
    half = 0.5 * v
    return half + half * jnp.tanh(half)


def stack_lanes(x):
    high, low = split(x)
    return jnp.concatenate([high, low, high], axis=1)


def beside(x):
    return jnp.concatenate(split(x), axis=1)


def mesh_weights_body(gain_ref, up_ref, down_ref, out_ref):
    out_ref[:, 0:256] = beside(up_ref[...].T * gain_ref[...])
    high, low = split(down_ref[...].T)
    out_ref[0:128, 256:512] = high
    out_ref[128:256, 256:512] = low


def prepare_body(pos_ref, long_ref, again_ref, aup_ref, adown_ref, out_ref, hat_out):
    out_ref[1024:1152, :] = beside((aup_ref[...].T * again_ref[...]).T)
    out_ref[1152:1408, 0:256] = beside(adown_ref[...])
    out_ref[1152:1280, 256:512] = beside(long_ref[...])
    pos = rows_of(pos_ref)
    high, low = split(planes_down(pos))
    main = 2 * LANES
    pieces = [high[:main], high[:main], low[:main], high[main : main + 64], high[main : main + 64], low[main:]]
    out_ref[0:1024, :] = jnp.concatenate(pieces, axis=0)
    ux = pos[0:1, :] * 8.0
    hats = [hat(ux - float(x)) for x in range(9)] + [jnp.zeros((7, ATOMS), F32)]
    hat_out[...] = jnp.concatenate(hats, axis=0)


def dot_beside(x, pair):
    high, low = split(x)
    width = pair.shape[1] // 2
    wide = dot(high, pair)
    return wide[:, :width] + (wide[:, width:] + dot(low, pair[:, :width]))


def final_body(msg_ref, in_ref, mesh_ref, set_ref, hat_ref, out_ref):
    mesh_out, stacks = [], []
    width = 12
    for r in range(0, ROWS, width):
        cells = jnp.concatenate(
            [in_ref[pl.ds(r + k, LANES, stride=ROWS), :] for k in range(width)], axis=1
        )
        inverse = lax.rsqrt(jnp.mean(cells * cells, axis=0, keepdims=True) + 1e-06)
        stacks.append(stack_rows(cells * inverse))
    first = mesh_ref[...]
    up = jnp.concatenate([first[:, :256], first[:, :128]], axis=1)
    down = jnp.concatenate([first[:128, 256:], first[128:, 256:], first[:128, 256:]], axis=1)
    for stack in stacks:
        result = dot(down, stack_rows(silu(dot(up, stack))))
        mesh_out += [result[:, k * LANES : (k + 1) * LANES] for k in range(width)]
    below = lane_iota((1, LANES)) < 64
    top = mesh_out[16:]
    mixed = lambda a, b: jnp.where(below, half_turn(a), b)
    edge = [mixed(top[0], top[1]), mixed(top[2], top[3]), half_turn(top[4])]
    stacks = []
    for x in range(9):
        first, second, last = edge if x == 8 else [mesh_out[x], mesh_out[8 + x], top[x]]
        high, low = split(jnp.concatenate([first, second], axis=1))
        rounded = last.astype(BF).astype(F32)
        both = jnp.where(below, rounded, half_turn(last - rounded))
        stacks.append(jnp.concatenate([high, low, high, both.astype(BF), rounded.astype(BF)], axis=1))
    found = dot(jnp.concatenate(stacks, axis=0), set_ref[0:1024, :])
    total = None
    for x in range(9):
        term = found[x * LANES : (x + 1) * LANES] * hat_ref[x : x + 1, :]
        total = term if total is None else total + term
    summed = msg_ref[...] + dot_beside(total.T, set_ref[1152:1280, 256:512])
    inverse = lax.rsqrt(jnp.mean(summed * summed, axis=1, keepdims=True) + 1e-06)
    hidden = silu(dot_beside(summed * inverse, set_ref[1024:1152, :]))
    out_ref[...] = summed + dot_beside(hidden, set_ref[1152:1408, 0:256])


def whole():
    return pl.BlockSpec(memory_space=pltpu.VMEM)


def scalars():
    return pl.BlockSpec(memory_space=pltpu.SMEM)


def in_hbm(x):
    return pltpu.with_memory_space_constraint(x, pltpu.HBM)


def remote():
    return pl.BlockSpec(memory_space=pltpu.HBM)


class Fetched:
    def __init__(self, source, target, semaphore, first, cuts):
        self.target = target
        self.copies = []
        for k, (low, high) in enumerate(zip(cuts[:-1], cuts[1:])):
            rows = pl.ds(low, high - low)
            copy = pltpu.make_async_copy(source.at[rows], target.at[rows], semaphore.at[first + k])
            copy.start()
            self.copies.append([low, high, copy])

    def __getitem__(self, index):
        rows = index[0] if isinstance(index, tuple) else index
        if isinstance(rows, slice):
            start, stop = rows.start or 0, self.target.shape[0] if rows.stop is None else rows.stop
        elif isinstance(rows, int):
            start, stop = rows, rows + 1
        else:
            start, stop = 0, self.target.shape[0]
        for entry in self.copies:
            if entry[2] is not None and entry[0] < stop and entry[1] > start:
                entry[2].wait()
                entry[2] = None
        return self.target[index]


def call(body, name, shapes, places, scratch, cost, operands, cuts={}):
    specs = {"v": whole, "s": scalars, "h": remote}
    far = [i for i, p in enumerate(places) if p == "h"]
    buffers = [pltpu.VMEM(operands[i].shape, operands[i].dtype) for i in far]
    count = len(places)
    parts = [cuts.get(i, (0, operands[i].shape[0])) for i in far]
    firsts = [sum(len(p) - 1 for p in parts[:k]) for k in range(len(far) + 1)]

    def kernel(*refs):
        inputs, rest = list(refs[:count]), refs[count:]
        if far:
            held, semaphores = rest[-len(far) - 1 : -1], rest[-1]
            for k, i in enumerate(far):
                inputs[i] = Fetched(inputs[i], held[k], semaphores, firsts[k], parts[k])
            rest = rest[: -len(far) - 1]
        body(*inputs, *rest)

    extra = buffers + [pltpu.SemaphoreType.DMA((firsts[-1],))] if far else []
    return pl.pallas_call(
        kernel,
        out_shape=[jax.ShapeDtypeStruct(x, F32) if isinstance(x, tuple) else x for x in shapes],
        in_specs=[specs[p]() for p in places],
        out_specs=[whole()] * len(shapes),
        scratch_shapes=list(scratch) + extra,
        name=name,
        compiler_params=pltpu.CompilerParams(vmem_limit_bytes=LIMIT),
        cost_estimate=pl.CostEstimate(flops=cost, bytes_accessed=4 * 1024 * 1024, transcendentals=0),
    )(*operands)


def spread_call(*operands):
    operands = [in_hbm(x) for x in operands]
    shapes = [(PACK, LANES), (LANES * ROWS, LANES)]
    return call(spread_body, "spread", shapes, "hhhh", [], 1_200_000_000, operands)


def prepare_call(*operands):
    shapes = [jax.ShapeDtypeStruct((1408, 512), BF), (16, ATOMS)]
    return call(prepare_body, "prepare", shapes, "v" * 5, [], PREPARE_COST, operands)


def first_table_extra():
    table = jnp.asarray(filter_tables()[:MESH])
    return Extra(copy_body, [jax.ShapeDtypeStruct(table.shape, BF)], (table,))


def copy_body(source_ref, target_ref):
    target_ref[...] = source_ref[...]


def filter_call(screening, smearing, received, first):
    scratch = [pltpu.VMEM((MESH * TURN, LANES), F32), pltpu.VMEM((256, LANES), F32)]
    operands = (screening, smearing, received, first, in_hbm(jnp.asarray(filter_tables())))
    shapes = [(LANES * ROWS, LANES)]
    return call(filter_body, "filter", shapes, "ssvvh", scratch, 2_000_000_000, operands)[0]


class Extra:
    def __init__(self, body, shapes, operands):
        self.body, self.shapes, self.operands = body, shapes, operands


def short_call(mesh, blocks, extra, live, pos, part, mix, *packs):
    with jax.sharding.use_abstract_mesh(mesh.abstract_mesh):
        units = [pltpu.ACC(i)((BASES // 2 * CHUNK, 2 * LANES), F32) for i in range(2)]
    scratch = [
        pltpu.VMEM((len(blocks), ATOMS + 64, 2 * LANES), BF),
        pltpu.VMEM((len(blocks), 2, 16, LANES), F32),
        pltpu.VMEM((3 * ATOMS, LANES), F32),
    ]
    body = functools.partial(short_body, blocks, units, len(packs), extra)
    operands = (live, pos, part, mix, *packs, *extra.operands)
    places = "s" + "v" * (len(operands) - 1)
    shapes = [(ATOMS, LANES)] + extra.shapes
    return call(body, "short_range", shapes, places, scratch, SHORT_COST, operands)


def final_call(messages, returned, mesh, weights, hats):
    operands = (messages, returned, mesh, in_hbm(weights), in_hbm(hats))
    cuts = {3: (0, 1024, 1408)}
    return call(final_body, "final", [(ATOMS, LANES)], "vvvhh", [], 2_400_000_000, operands, cuts)[0]


def passed_along(array, axis, by):
    count = lax.axis_size(axis)
    return lax.ppermute(array, axis, [(i, (i + by) % count) for i in range(count)])


def on_device(
    mesh,
    features,
    positions,
    tile_lists,
    value_proj,
    radial_mix,
    charge_proj,
    screening,
    smearing,
    mesh_gain,
    mesh_up,
    mesh_down,
    long_proj,
    atom_gain,
    atom_up,
    atom_down,
):
    feat, pos = features[0, 0], positions.reshape(3, 1, ATOMS)
    everyone = ("wide", "sixteen")
    packed, spread = spread_call(pos, feat, charge_proj, value_proj)
    below = passed_along(packed, "sixteen", 1)
    above = passed_along(packed, "sixteen", -1)
    received = lax.all_to_all(spread, everyone, split_axis=0, concat_axis=0, tiled=True)
    near = jnp.concatenate([below, packed, above], axis=0)
    left = passed_along(near, "wide", 1)
    right = passed_along(near, "wide", -1)
    codes = jnp.arange(36, dtype=jnp.int32)
    live = jnp.any(tile_lists[0, 0][:, :, None] == codes, axis=1).astype(jnp.int32)
    prepared = prepare_call(pos, long_proj, atom_gain[None], atom_up, atom_down)
    part, table = short_call(mesh, (3, 4, 5), first_table_extra(), live, pos, feat, radial_mix, near)
    received, part, table = lax.optimization_barrier((received, part, table))
    filtered = filter_call(screening, smearing, received, table)
    returned = lax.all_to_all(filtered, everyone, split_axis=0, concat_axis=0, tiled=True)
    shape = jax.ShapeDtypeStruct((256, 512), BF)
    weights = Extra(mesh_weights_body, [shape], (mesh_gain[None], mesh_up, mesh_down))
    messages, mesh_weights = short_call(
        mesh, (0, 1, 2, 6, 7, 8), weights, live, pos, part, radial_mix, left, right
    )
    updated = final_call(messages, returned, mesh_weights, *prepared)
    return updated[None, None]


def solution(mesh):
    block = P("wide", "sixteen", None, None)
    channel = P(("wide", "sixteen"))
    in_specs = (block,) * 3 + (P(),) * 3 + (channel,) * 2 + (P(),) * 7
    return jax.shard_map(
        functools.partial(on_device, mesh), mesh=mesh, in_specs=in_specs, out_specs=block, check_vma=False
    )
```
